128 devices in a mesh: silo: 8 (over z, core), row: 16 (over y, x).
Axes of the slice: x: 4, y: 4, z: 4, core: 2. Of those that a mesh axis runs over, the one named last changes fastest.
Arguments:
- silo_grams: float32 [16, 4096, 4096], P('silo', 'row'), may hold values from -9 to 81, as said below
- silo_weights: bfloat16 [16, 4096, 640], P('silo', 'row'), may hold values from -6 to 6
Outputs:
- merged_rows: float32 [640, 4096], P(('silo', 'row'))
The draws below stay inside these ranges and needn't reach their ends.
Inputs may be any that keep to these rules, and one draw needn't show every extreme that they name: `silo_grams`: each silo's Gram is symmetric up to float32 rounding and positive definite.
All inputs are finite; a program needn't handle non-finite values.
Results may differ from the reference program's by a relative error of at most 0.0003.
Values may be sent and summed in bfloat16 or wider, within the bound.
A program may use at most 128 MiB of HBM per device.

```python
import math
import jax
import jax.numpy as jnp
from jax import lax

D = 4096
C = 640
ITERS = 2
SILOS = 16


def noise_matrix(noise_key):
    raw_noise = jnp.clip(jax.random.normal(noise_key, (D, D), jnp.float32), -4.0, 4.0)
    return (raw_noise + raw_noise.T) * (0.45 / (2.0 * math.sqrt(2.0 * D)))


def draw_silo_grams(key, part):
    key_scale, key_common, key_silos = jax.random.split(jax.random.fold_in(key, 17), 3)
    row_trend = 1.0 + 2.0 * jnp.arange(D, dtype=jnp.float32) / D
    row_scale = row_trend * jnp.exp(jax.random.uniform(key_scale, (D,), jnp.float32, 0.0, math.log(2.0)))
    common_part = noise_matrix(key_common)

    def single_silo(silo_key):
        key_level, key_own = jax.random.split(silo_key)
        silo_level = jax.random.uniform(key_level, (D,), jnp.float32, 1.0, 2.0)
        silo_matrix = common_part + noise_matrix(key_own) + jnp.diag(silo_level)
        return row_scale[:, None] * silo_matrix * row_scale[None, :]
    return lax.map(single_silo, jax.random.split(key_silos, SILOS))


def shard_levels(rng, dims, cuts, least, high):
    factor_of = 1.0
    for dim, shards_of in cuts:
        heights = jax.random.uniform(jax.random.fold_in(jax.random.fold_in(rng, 6), dim), (shards_of,), jnp.float32, least / len(cuts), high / len(cuts))
        factor_of = factor_of * jnp.repeat(jnp.exp(heights), dims[dim] // shards_of).reshape((-1,) + (1,) * (len(dims) - 1 - dim))
    return factor_of


def bell_draw(key, extent, scale, bound, cuts=(), kind=jnp.bfloat16):
    drawn = jax.random.normal(key, extent, jnp.float32) * scale
    if len(cuts) > 0:
        drawn = shard_levels(key, extent, cuts, -0.22, 0.18) * drawn
    return jnp.clip(drawn, min=-bound, max=bound).astype(kind)


def setup_inputs(seed: int = 0) -> dict:
    seeds = jax.random.split(jax.random.key(seed), 3)
    silo_grams = draw_silo_grams(jax.random.fold_in(seeds[2], 71), 0)
    silo_weights = bell_draw(seeds[1], (SILOS, D, C), 1.0, 6.0, ((0, 8), (1, 16)))
    return dict(silo_grams=silo_grams, silo_weights=silo_weights)


full_precision = lax.Precision.HIGHEST

def conj_grad(right_side, operator):
    solution = jnp.zeros_like(right_side)
    residual = right_side
    direction = right_side
    res_norm = lax.optimization_barrier(jnp.sum(residual * residual, axis=0))
    for iteration in range(ITERS):
        mapped = jnp.dot(operator, direction, precision=full_precision)
        step_size = res_norm / lax.optimization_barrier(jnp.sum(direction * mapped, axis=0))
        solution = solution + step_size * direction
        residual = residual - step_size * mapped
        next_norm = lax.optimization_barrier(jnp.sum(residual * residual, axis=0))
        direction = residual + next_norm / res_norm * direction
        res_norm = next_norm
    return solution

def reference(silo_grams, silo_weights):
    operator = lax.optimization_barrier(jnp.sum(silo_grams, axis=0))

    def add_silo(running, paired):
        silo_gram, silo_weight = paired
        return (running + jnp.dot(silo_gram, silo_weight.astype(jnp.float32), precision=full_precision), None)
    right_side, unused = lax.scan(add_silo, jnp.zeros((D, C), jnp.float32), (silo_grams, silo_weights))
    solution = conj_grad(right_side, operator)
    return solution.T
```

```python
import jax
import jax.numpy as jnp
from jax import lax
from jax.experimental import pallas as pl
from jax.experimental.pallas import tpu as pltpu
from jax.sharding import Mesh
from jax.sharding import PartitionSpec as P

F32, BF16 = jnp.float32, jnp.bfloat16
MESH = pl.DeviceIdType.MESH
AXES = ("z", "core", "y", "x")
NT = (((1,), (1,)), ((), ()))
NN = (((1,), (0,)), ((), ()))
NEAR = (1, 3, 2)


def dot(a, b, dims=NN, precision=None):
    return lax.dot_general(a, b, dims, precision=precision, preferred_element_type=F32)


def halves(value):
    high = value.astype(BF16)
    return high, (value - high.astype(F32)).astype(BF16)


def kernel(
    g_hbm, w_ref, out_ref,
    g, gh, gl, wt, p, q, r, far, near, second, third,
    ap, a_sib, a_rs, a_op, bg, qg, pg, tiny,
    load_sem, s_sib, r_sib, s_one, r_one, s_two, r_two, s_z, r_z,
    s_asib, r_asib, s_ars, r_ars, s_aag, r_aag, s_afw, r_afw,
    s_b, r_b, s_q, r_q, s_t, r_t,
):
    z, k, y, x = (lax.axis_index(a) for a in AXES)

    def dxy(i, j):
        return (1 - k) * i + k * j, (1 - k) * j + k * i

    def block_row(i, j):
        dx, dy = dxy(i, j)
        return lax.rem(y + dy, 4) * 4 + lax.rem(x + dx, 4)

    def canon(i, j):
        dx, dy = dxy(i, j)
        return dx * 4 + dy

    def plane_peer(i, j):
        dx, dy = dxy(i, j)
        return (z, k, lax.rem(y + dy, 4), lax.rem(x + dx, 4))

    def z_peer(d):
        return (lax.rem(z + d, 4), k, y, x)

    sibling = (z, 1 - k, y, x)

    def remote(src, dst, ssem, rsem, device):
        return pltpu.make_async_remote_copy(src, dst, ssem, rsem, device_id=device, device_id_type=MESH)

    sent = []

    def send(*args):
        copy = remote(*args)
        copy.start()
        sent.append(copy)

    def arrived(dst, ssem, rsem):
        remote(dst, dst, ssem, rsem, sibling).wait_recv()

    barrier = pltpu.get_barrier_semaphore()
    others = [(i, j) for i in range(4) for j in range(4) if i or j]
    for i, j in others:
        pl.semaphore_signal(barrier, 1, device_id=plane_peer(i, j), device_id_type=MESH)
    for d in NEAR:
        pl.semaphore_signal(barrier, 1, device_id=z_peer(d), device_id_type=MESH)
    pl.semaphore_signal(barrier, 1, device_id=sibling, device_id_type=MESH)

    def load(i, j):
        col = pl.multiple_of(block_row(i, j) * 256, 256)
        return pltpu.make_async_copy(g_hbm.at[:, :, pl.ds(col, 256)], g.at[4 * i + j], load_sem.at[4 * i + j])

    order = [(i, 2) for i in range(4)] + [(2, j) for j in (0, 1, 3)]
    order += [(i, j) for j in (1, 3) for i in (0, 1, 3)] + [(1, 0), (3, 0), (0, 0)]
    for i, j in order:
        load(i, j).start()

    flipped = w_ref[...].reshape(512, 640).astype(F32).T.astype(BF16)
    for s in range(8):
        wt[s % 2, s // 2] = flipped[s * 80 : (s + 1) * 80]

    def split(i, j):
        load(i, j).wait()
        value = g[4 * i + j]
        high, low = halves(value)
        gh[4 * i + j] = high.reshape(512, 256)
        gl[4 * i + j] = low.reshape(512, 256)
        ap[canon(i, j)] = value[0] + value[1]

    def tile(core, slot):
        w = wt[core].reshape(320, 512)
        return (dot(w, gh[slot]) + dot(w, gl[slot])).reshape(4, 80, 256)

    def for_sibling(m):
        def body(n, carry):
            q[4 * m + n] = tile(1 - k, 4 * n + m)
            return carry

        lax.fori_loop(0, 4, body, 0)
        rows = pl.ds(4 * m, 4)
        send(q.at[rows], r.at[rows], s_sib.at[m], r_sib.at[m], sibling)

    def for_self(m):
        def body(n, carry):
            p[4 * m + n] = tile(k, 4 * m + n)
            return carry

        lax.fori_loop(0, 4, body, 0)

    def add_sibling(m):
        rows = pl.ds(4 * m, 4)
        arrived(r.at[rows], s_sib.at[m], r_sib.at[m])

        def body(n, carry):
            p[4 * m + n] += r[4 * m + n]
            return carry

        lax.fori_loop(0, 4, body, 0)

    up, down = plane_peer(1, 0), plane_peer(3, 0)

    for i in range(4):
        split(i, 2)
    pl.semaphore_wait(barrier, 19)
    for_sibling(2)
    for j in (0, 1, 3):
        split(2, j)
    for_self(2)
    add_sibling(2)
    send(p.at[pl.ds(8, 2)], far.at[0], s_one.at[0], r_one.at[0], up)
    send(p.at[pl.ds(10, 2)], far.at[1], s_one.at[1], r_one.at[1], down)
    for j in (1, 3):
        for i in (0, 1, 3):
            split(i, j)
        for_sibling(j)
    for i in (1, 3):
        split(i, 0)
    for_self(1)
    add_sibling(1)
    send(p.at[pl.ds(6, 2)], near.at[0, 1], s_one.at[2], r_one.at[2], up)
    for_self(3)
    add_sibling(3)
    send(p.at[pl.ds(12, 2)], near.at[1, 0], s_one.at[3], r_one.at[3], down)
    split(0, 0)

    mine, theirs = pl.ds(8 * k, 8), pl.ds(8 * (1 - k), 8)
    send(ap.at[theirs], a_sib, s_asib.at[0], r_asib.at[0], sibling)
    for_sibling(0)
    for_self(0)
    arrived(a_sib, s_asib.at[0], r_asib.at[0])

    def add_op(n, carry):
        a_sib[n] += ap[8 * k + n]
        return carry

    lax.fori_loop(0, 8, add_op, 0)
    for d in NEAR:
        at = pl.ds(2 * lax.rem(z + d, 4), 2)
        send(a_sib.at[at], a_rs.at[3 - d], s_ars.at[3 - d], r_ars.at[3 - d], z_peer(d))
    add_sibling(0)

    arrived(far.at[0], s_one.at[0], r_one.at[0])
    for n in range(2):
        p[4 + n] += far[0, n]
    send(p.at[pl.ds(4, 2)], near.at[0, 0], s_one.at[4], r_one.at[4], up)
    arrived(far.at[1], s_one.at[1], r_one.at[1])
    for n in range(2):
        p[14 + n] += far[1, n]
    send(p.at[pl.ds(14, 2)], near.at[1, 1], s_one.at[5], r_one.at[5], down)

    for d in NEAR:
        arrived(a_rs.at[3 - d], s_ars.at[3 - d], r_ars.at[3 - d])
    own = 8 * k + 2 * z
    for n in range(2):
        total = a_sib[2 * z + n] + a_rs[0, n] + a_rs[1, n] + a_rs[2, n]
        high, low = halves(total)
        a_op[own + n, 0] = high
        a_op[own + n, 1] = low
    for d in NEAR:
        at = pl.ds(own, 2)
        send(a_op.at[at], a_op.at[at], s_aag.at[3 - d], r_aag.at[3 - d], z_peer(d))
    send(a_op.at[pl.ds(own, 2)], a_op.at[pl.ds(own, 2)], s_afw.at[0], r_afw.at[0], sibling)

    arrived(near.at[0, 1], s_one.at[2], r_one.at[2])
    arrived(near.at[1, 0], s_one.at[3], r_one.at[3])
    arrived(near.at[0, 0], s_one.at[4], r_one.at[4])
    arrived(near.at[1, 1], s_one.at[5], r_one.at[5])
    for h in (1, 0):
        for n in range(2):
            p[2 * h + n] += near[0, h, n] + near[1, h, n]

    for d in NEAR:
        send(p.at[d], second.at[3 - d], s_two.at[3 - d], r_two.at[3 - d], plane_peer(0, d))
    for d in NEAR:
        arrived(second.at[3 - d], s_two.at[3 - d], r_two.at[3 - d])
    p[0] += second[0] + second[1] + second[2]

    for d in NEAR:
        send(p.at[0, lax.rem(z + d, 4)], third.at[3 - d], s_z.at[3 - d], r_z.at[3 - d], z_peer(d))
    for d in NEAR:
        arrived(third.at[3 - d], s_z.at[3 - d], r_z.at[3 - d])
    right = p[0, z] + third[0] + third[1] + third[2]

    def gather(buf, value, ss, rs, use):
        high, low = halves(value)
        buf[0, 0:80] = high
        buf[0, 80:160] = low
        for d in NEAR:
            send(buf.at[0], buf.at[16 - 4 * d], ss.at[16 - 4 * d], rs.at[16 - 4 * d], plane_peer(d, 0))
            send(buf.at[0], buf.at[4 - d], ss.at[4 - d], rs.at[4 - d], plane_peer(0, d))
        use(0, 0)
        for i in NEAR:
            arrived(buf.at[4 * i], ss.at[4 * i], rs.at[4 * i])
            for d in NEAR:
                at = 4 * i + 4 - d
                send(buf.at[4 * i], buf.at[at], ss.at[at], rs.at[at], plane_peer(0, d))
        for i in NEAR:
            use(i, 0)
        for i in (0, 1, 3, 2):
            for j in NEAR:
                at = 4 * i + j
                arrived(buf.at[at], ss.at[at], rs.at[at])
                use(i, j)

    def whole(buf, slot):
        return buf[slot, 0:80].astype(F32) + buf[slot, 80:160].astype(F32)

    def apply_op(buf):
        def body(n, total):
            i, j = n // 4, n % 4
            at = canon(i, j)
            wide = dot(buf[n], a_op[at, 0], NT)
            return total + wide[0:80] + wide[80:160] + dot(buf[n, 0:80], a_op[at, 1], NT)

        return lax.fori_loop(0, 16, body, jnp.zeros((80, 256), F32))

    gather(bg, right, s_b, r_b, lambda i, j: None)

    for d in NEAR:
        at = pl.ds(8 * k + 2 * lax.rem(z + d, 4), 2)
        arrived(a_op.at[at], s_aag.at[d - 1], r_aag.at[d - 1])
        send(a_op.at[at], a_op.at[at], s_afw.at[d], r_afw.at[d], sibling)
    for d in range(4):
        at = pl.ds(8 * (1 - k) + 2 * lax.rem(z + d, 4), 2)
        arrived(a_op.at[at], s_afw.at[d], r_afw.at[d])

    mapped = apply_op(bg)
    gather(qg, mapped, s_q, r_q, lambda i, j: None)

    zero = jnp.zeros((80, 256), F32)

    def sums(n, carry):
        b, m = whole(bg, n), whole(qg, n)
        return carry[0] + b * b, carry[1] + b * m

    norm, curv = lax.fori_loop(0, 16, sums, (zero, zero))
    norm = jnp.sum(norm, axis=1, keepdims=True)
    step = norm / jnp.sum(curv, axis=1, keepdims=True)

    def residuals(n, total):
        res = whole(bg, n) - step * whole(qg, n)
        return total + res * res

    beta = jnp.sum(lax.fori_loop(0, 16, residuals, zero), axis=1, keepdims=True) / norm

    def directions(n, carry):
        b = whole(bg, n)
        high, low = halves(b - step * whole(qg, n) + beta * b)
        pg[n, 0:80] = high
        pg[n, 80:160] = low
        return carry

    lax.fori_loop(0, 16, directions, 0)
    product = whole(pg, 0) * apply_op(pg)
    product = jnp.concatenate([product, jnp.zeros((48, 256), F32)], axis=0)
    tiny[0] = dot(jnp.ones((8, 256), F32), product, NT, lax.Precision.HIGHEST)
    for i, j in others:
        at = (4 - i) % 4 * 4 + (4 - j) % 4
        send(tiny.at[0], tiny.at[at], s_t.at[at], r_t.at[at], plane_peer(i, j))

    first = 5 * (4 * y + x)
    line = lax.broadcasted_iota(jnp.int32, (16, 80), 0)
    column = lax.broadcasted_iota(jnp.int32, (16, 80), 1)
    pick = jnp.where((line < 5) & (column == line + first), 1.0, 0.0).astype(BF16)

    def picked(buf, n):
        return (dot(pick, buf[n, 0:80]) + dot(pick, buf[n, 80:160]))[0:8]

    bs = [picked(bg, n) for n in range(16)]
    ms = [picked(qg, n) for n in range(16)]

    def row_sum(parts):
        total = parts[0]
        for part in parts[1:]:
            total = total + part
        return jnp.sum(total, axis=1, keepdims=True)

    norm5 = row_sum([b * b for b in bs])
    step5 = norm5 / row_sum([b * m for b, m in zip(bs, ms)])
    rs = [b - step5 * m for b, m in zip(bs, ms)]
    next5 = row_sum([v * v for v in rs])
    ps = [v + next5 / norm5 * b for v, b in zip(rs, bs)]

    for i, j in others:
        at = 4 * i + j
        arrived(tiny.at[at], s_t.at[at], r_t.at[at])
    curv = tiny[0]
    for n in range(1, 16):
        curv = curv + tiny[n]
    line = lax.broadcasted_iota(jnp.int32, (8, 128), 0)
    column = lax.broadcasted_iota(jnp.int32, (8, 128), 1)
    curv = jnp.sum(jnp.where(column == line + first, curv, 0.0), axis=1, keepdims=True)
    step2 = next5 / curv
    for i in range(4):
        for j in range(4):
            n = 4 * i + j
            value = step5 * bs[n] + step2 * ps[n]
            col = pl.multiple_of(block_row(i, j) * 256, 256)
            out_ref[:, pl.ds(col, 256)] = value[0:5]
    for copy in sent:
        copy.wait_send()


def local(silo_grams, silo_weights):
    dma = pltpu.SemaphoreType.DMA
    scratch = [
        pltpu.VMEM((16, 2, 256, 256), F32),
        pltpu.VMEM((16, 512, 256), BF16),
        pltpu.VMEM((16, 512, 256), BF16),
        pltpu.VMEM((2, 4, 80, 512), BF16),
        pltpu.VMEM((16, 4, 80, 256), F32),
        pltpu.VMEM((16, 4, 80, 256), F32),
        pltpu.VMEM((16, 4, 80, 256), F32),
        pltpu.VMEM((2, 2, 4, 80, 256), F32),
        pltpu.VMEM((2, 2, 2, 4, 80, 256), F32),
        pltpu.VMEM((3, 4, 80, 256), F32),
        pltpu.VMEM((3, 80, 256), F32),
        pltpu.VMEM((16, 256, 256), F32),
        pltpu.VMEM((8, 256, 256), F32),
        pltpu.VMEM((3, 2, 256, 256), F32),
        pltpu.VMEM((16, 2, 256, 256), BF16),
        pltpu.VMEM((16, 160, 256), BF16),
        pltpu.VMEM((16, 160, 256), BF16),
        pltpu.VMEM((16, 160, 256), BF16),
        pltpu.VMEM((16, 8, 128), F32),
    ]
    counts = [16, 4, 4, 6, 6, 3, 3, 3, 3, 1, 1, 3, 3, 3, 3, 4, 4, 16, 16, 16, 16, 16, 16]
    scratch += [dma((n,)) for n in counts]
    return pl.pallas_call(
        kernel,
        out_shape=jax.ShapeDtypeStruct((5, 4096), F32),
        in_specs=[pl.BlockSpec(memory_space=pl.ANY), pl.BlockSpec(memory_space=pltpu.VMEM)],
        out_specs=pl.BlockSpec(memory_space=pltpu.VMEM),
        scratch_shapes=scratch,
        compiler_params=pltpu.CompilerParams(collective_id=0, has_side_effects=True, vmem_limit_bytes=62 << 20),
        cost_estimate=pl.CostEstimate(flops=6_500_000_000, bytes_accessed=9_200_000, transcendentals=0),
    )(silo_grams, silo_weights)


def solution(mesh):
    torus = Mesh(mesh.devices.reshape(4, 2, 4, 4), AXES)
    silo, row = ("z", "core"), ("y", "x")
    in_specs = (P(silo, row, None), P(silo, row, None))
    out_specs = P(silo + row, None)
    return jax.shard_map(local, mesh=torus, in_specs=in_specs, out_specs=out_specs, check_vma=False)
```

```python
import jax
import jax.numpy as jnp
from jax import lax
from jax.experimental import pallas as pl
from jax.experimental.pallas import tpu as pltpu
from jax.sharding import Mesh
from jax.sharding import PartitionSpec as P

F32, BF16 = jnp.float32, jnp.bfloat16
MESH = pl.DeviceIdType.MESH
AXES = ("z", "core", "y", "x")
NT = (((1,), (1,)), ((), ()))
NN = (((1,), (0,)), ((), ()))
NEAR = (1, 3, 2)
FAR = (2, 1, 3, 0)


def dot(a, b, dims=NN, precision=None):
    return lax.dot_general(a, b, dims, precision=precision, preferred_element_type=F32)


def halves(value):
    high = value.astype(BF16)
    return high, (value - high.astype(F32)).astype(BF16)


def kernel(
    g_hbm, w_hbm, out_ref,
    w_raw, g, gh, gl, wt, p, q, r, far, near, second, third,
    ap, a_sib, a_far, a_near, a_op, bg, qg, pg, tiny,
    w_sem, load_sem, s_sib, r_sib, s_one, r_one, s_two, r_two, s_z, r_z,
    s_asib, r_asib, s_ars, r_ars, s_aag, r_aag, s_afw, r_afw,
    s_b, r_b, s_q, r_q, s_t, r_t,
):
    z, k, y, x = (lax.axis_index(a) for a in AXES)

    def dxy(i, j):
        return (1 - k) * i + k * j, (1 - k) * j + k * i

    def block_row(i, j):
        dx, dy = dxy(i, j)
        return lax.rem(y + dy, 4) * 4 + lax.rem(x + dx, 4)

    def canon(i, j):
        dx, dy = dxy(i, j)
        return dx * 4 + dy

    def plane_peer(i, j):
        dx, dy = dxy(i, j)
        return (z, k, lax.rem(y + dy, 4), lax.rem(x + dx, 4))

    def z_peer(d):
        return (lax.rem(z + d, 4), k, y, x)

    sibling = (z, 1 - k, y, x)

    def remote(src, dst, ssem, rsem, device):
        return pltpu.make_async_remote_copy(src, dst, ssem, rsem, device_id=device, device_id_type=MESH)

    sent = []

    def send(*args):
        copy = remote(*args)
        copy.start()
        sent.append(copy)

    def arrived(dst, rsem):
        remote(dst, dst, s_sib.at[0], rsem, sibling).wait_recv()

    weights = pltpu.make_async_copy(w_hbm, w_raw, w_sem.at[0])
    weights.start()

    def load(i, j):
        col = pl.multiple_of(block_row(i, j) * 256, 256)
        return pltpu.make_async_copy(g_hbm.at[:, :, pl.ds(col, 256)], g.at[4 * i + j], load_sem.at[4 * i + j])

    early = [(i, 2) for i in range(4)] + [(2, j) for j in (0, 1, 3)]
    late = [(i, j) for j in (1, 3) for i in (0, 1, 3)] + [(1, 0), (3, 0), (0, 0)]
    for i, j in early + late:
        load(i, j).start()

    barrier = pltpu.get_barrier_semaphore()
    others = [(i, j) for i in FAR for j in FAR if i or j]
    for i, j in others:
        pl.semaphore_signal(barrier, 1, device_id=plane_peer(i, j), device_id_type=MESH)
    for d in NEAR:
        pl.semaphore_signal(barrier, 1, device_id=z_peer(d), device_id_type=MESH)
    pl.semaphore_signal(barrier, 1, device_id=sibling, device_id_type=MESH)

    weights.wait()
    flipped = w_raw[...].reshape(512, 640).astype(F32).T.astype(BF16)
    for s in range(8):
        wt[s % 2, lax.rem(s // 2 + 4 - z, 4)] = flipped[s * 80 : (s + 1) * 80]

    def split(i, j):
        load(i, j).wait()
        value = g[4 * i + j]
        high, low = halves(value)
        gh[4 * i + j] = high.reshape(512, 256)
        gl[4 * i + j] = low.reshape(512, 256)
        ap[canon(i, j)] = value[0] + value[1]

    def tile(core, slot):
        w = wt[core].reshape(320, 512)
        return (dot(w, gh[slot]) + dot(w, gl[slot])).reshape(4, 80, 256)

    def loop(count, step):
        def body(n, carry):
            step(n)
            return carry

        lax.fori_loop(0, count, body, 0)

    def for_sibling(m, lo, count, sem):
        def step(n):
            q[4 * m + lo + n] = tile(1 - k, 4 * (lo + n) + m)

        loop(count, step)
        rows = pl.ds(4 * m + lo, count)
        send(q.at[rows], r.at[rows], s_sib.at[sem], r_sib.at[sem], sibling)

    def for_self(m, lo, count):
        def step(n):
            p[4 * m + lo + n] = tile(k, 4 * m + lo + n)

        loop(count, step)

    def add_sibling(m, lo, count, sem):
        rows = pl.ds(4 * m + lo, count)
        arrived(r.at[rows], r_sib.at[sem])

        def step(n):
            p[4 * m + lo + n] += r[4 * m + lo + n]

        loop(count, step)

    up, down = plane_peer(1, 0), plane_peer(3, 0)

    split(0, 2)
    split(1, 2)
    pl.semaphore_wait(barrier, 19)
    for_sibling(2, 0, 2, 0)
    split(2, 2)
    split(3, 2)
    for_sibling(2, 2, 2, 1)
    split(2, 0)
    split(2, 1)
    for_self(2, 0, 2)
    add_sibling(2, 0, 2, 0)
    send(p.at[pl.ds(8, 2)], far.at[0], s_one.at[0], r_one.at[0], up)
    split(2, 3)
    for_self(2, 2, 2)
    add_sibling(2, 2, 2, 1)
    send(p.at[pl.ds(10, 2)], far.at[1], s_one.at[1], r_one.at[1], down)

    for i, j in late:
        split(i, j)
    mine, theirs = pl.ds(8 * k, 8), pl.ds(8 * (1 - k), 8)
    send(ap.at[theirs], a_sib, s_asib.at[0], r_asib.at[0], sibling)

    for_sibling(1, 0, 4, 2)
    for_self(1, 0, 4)
    for_sibling(3, 0, 4, 3)
    add_sibling(1, 0, 4, 2)
    send(p.at[pl.ds(6, 2)], near.at[0, pl.ds(2, 2)], s_one.at[2], r_one.at[2], up)
    for_self(3, 0, 4)
    add_sibling(3, 0, 4, 3)
    send(p.at[pl.ds(12, 2)], near.at[1, pl.ds(0, 2)], s_one.at[3], r_one.at[3], down)

    arrived(a_sib, r_asib.at[0])

    def add_op(n):
        a_sib[n] += ap[8 * k + n]

    loop(8, add_op)

    def quarter(d, n):
        return 2 * lax.rem(z + d, 4) + n

    z_up, z_down = z_peer(1), z_peer(3)
    send(a_sib.at[quarter(2, 0)], a_far.at[0], s_ars.at[0], r_ars.at[0], z_up)
    send(a_sib.at[quarter(2, 1)], a_far.at[1], s_ars.at[1], r_ars.at[1], z_down)
    send(a_sib.at[quarter(1, 1)], a_near.at[0, 1], s_ars.at[2], r_ars.at[2], z_up)
    send(a_sib.at[quarter(3, 0)], a_near.at[1, 0], s_ars.at[3], r_ars.at[3], z_down)
    for_sibling(0, 0, 4, 4)
    for_self(0, 0, 4)
    add_sibling(0, 0, 4, 4)

    arrived(far.at[0], r_one.at[0])
    for n in (1, 0):
        p[4 + n] += far[0, n]
        send(p.at[4 + n], near.at[0, n], s_one.at[4 + n], r_one.at[4 + n], up)
    arrived(far.at[1], r_one.at[1])
    for n in range(2):
        p[14 + n] += far[1, n]
        send(p.at[14 + n], near.at[1, 2 + n], s_one.at[6 + n], r_one.at[6 + n], down)

    arrived(a_far.at[0], r_ars.at[0])
    a_sib[quarter(1, 0)] += a_far[0]
    send(a_sib.at[quarter(1, 0)], a_near.at[0, 0], s_ars.at[4], r_ars.at[4], z_up)
    arrived(a_far.at[1], r_ars.at[1])
    a_sib[quarter(3, 1)] += a_far[1]
    send(a_sib.at[quarter(3, 1)], a_near.at[1, 1], s_ars.at[5], r_ars.at[5], z_down)

    def second_axis(d):
        send(p.at[d, pl.ds(1, 3)], second.at[3 - d, pl.ds(1, 3)], s_two.at[3 - d], r_two.at[3 - d], plane_peer(0, d))
        send(p.at[d, 0], second.at[3 - d, 0], s_two.at[6 - d], r_two.at[6 - d], plane_peer(0, d))

    def whole_sum(n):
        p[n] += near[0, n] + near[1, n]

    arrived(near.at[0, pl.ds(2, 2)], r_one.at[2])
    arrived(near.at[1, pl.ds(0, 2)], r_one.at[3])
    arrived(near.at[0, 1], r_one.at[5])
    whole_sum(1)
    second_axis(1)
    arrived(near.at[1, 2], r_one.at[6])
    whole_sum(2)
    second_axis(2)
    arrived(near.at[1, 3], r_one.at[7])
    whole_sum(3)
    second_axis(3)
    arrived(near.at[0, 0], r_one.at[4])
    whole_sum(0)

    arrived(a_near.at[0, 1], r_ars.at[2])
    arrived(a_near.at[1, 0], r_ars.at[3])
    arrived(a_near.at[0, 0], r_ars.at[4])
    arrived(a_near.at[1, 1], r_ars.at[5])

    def op_rows(d):
        return pl.ds(8 * k + quarter(d, 0), 2)

    own = 8 * k + quarter(0, 0)
    for n in range(2):
        high, low = halves(a_sib[quarter(0, n)] + a_near[0, n] + a_near[1, n])
        a_op[own + n, 0] = high
        a_op[own + n, 1] = low
    send(a_op.at[op_rows(0)], a_op.at[op_rows(0)], s_aag.at[0], r_aag.at[0], z_up)
    send(a_op.at[op_rows(0)], a_op.at[op_rows(0)], s_aag.at[1], r_aag.at[1], z_down)
    send(a_op.at[op_rows(0)], a_op.at[op_rows(0)], s_afw.at[0], r_afw.at[0], sibling)

    for d in NEAR:
        arrived(second.at[3 - d, pl.ds(1, 3)], r_two.at[3 - d])
    for d in NEAR:
        p[0, d] += second[0, d] + second[1, d] + second[2, d]
        send(p.at[0, d], third.at[3 - d], s_z.at[3 - d], r_z.at[3 - d], z_peer(d))
    for d in NEAR:
        arrived(second.at[3 - d, 0], r_two.at[6 - d])
    right = p[0, 0] + second[0, 0] + second[1, 0] + second[2, 0]

    arrived(a_op.at[op_rows(3)], r_aag.at[0])
    at = 8 * k + quarter(3, 0)
    send(a_op.at[at], a_op.at[at], s_aag.at[2], r_aag.at[2], z_up)
    send(a_op.at[op_rows(3)], a_op.at[op_rows(3)], s_afw.at[1], r_afw.at[1], sibling)
    arrived(a_op.at[op_rows(1)], r_aag.at[1])
    at = 8 * k + quarter(1, 1)
    send(a_op.at[at], a_op.at[at], s_aag.at[3], r_aag.at[3], z_down)
    send(a_op.at[op_rows(1)], a_op.at[op_rows(1)], s_afw.at[2], r_afw.at[2], sibling)

    for d in NEAR:
        arrived(third.at[3 - d], r_z.at[3 - d])
    right = right + third[0] + third[1] + third[2]

    def spread(buf, value, ss, rs):
        high, low = halves(value)
        buf[0, 0:80] = high
        buf[0, 80:160] = low
        for d in NEAR:
            send(buf.at[0], buf.at[16 - 4 * d], ss.at[16 - 4 * d], rs.at[16 - 4 * d], plane_peer(d, 0))
        for d in NEAR:
            send(buf.at[0], buf.at[4 - d], ss.at[4 - d], rs.at[4 - d], plane_peer(0, d))

    def pass_on(buf, ss, rs):
        for i in NEAR:
            arrived(buf.at[4 * i], rs.at[4 * i])
            for d in NEAR:
                at = 4 * i + 4 - d
                send(buf.at[4 * i], buf.at[at], ss.at[at], rs.at[at], plane_peer(0, d))

    def collect(buf, rs, use):
        for i in range(4):
            use(4 * i)
        for i in (0, 1, 3, 2):
            for j in NEAR:
                at = 4 * i + j
                arrived(buf.at[at], rs.at[at])
                use(at)

    def whole(buf, slot):
        return buf[slot, 0:80].astype(F32) + buf[slot, 80:160].astype(F32)

    def op_term(buf, n):
        at = canon(n // 4, n % 4)
        wide = dot(buf[n], a_op[at, 0], NT)
        return wide[0:80] + wide[80:160] + dot(buf[n, 0:80], a_op[at, 1], NT)

    zero = jnp.zeros((80, 256), F32)
    spread(bg, right, s_b, r_b)
    pass_on(bg, s_b, r_b)

    for n in range(2):
        at = 8 * k + quarter(2, n)
        arrived(a_op.at[at], r_aag.at[2 + n])
        send(a_op.at[at], a_op.at[at], s_afw.at[3 + n], r_afw.at[3 + n], sibling)
    theirs = 8 * (1 - k)
    for n, d in enumerate((0, 3, 1)):
        arrived(a_op.at[pl.ds(theirs + quarter(d, 0), 2)], r_afw.at[n])
    for n in range(2):
        arrived(a_op.at[theirs + quarter(2, n)], r_afw.at[3 + n])

    total = [zero, zero]

    def use_right(n):
        total[0] = total[0] + op_term(bg, n)
        b = whole(bg, n)
        total[1] = total[1] + b * b

    collect(bg, r_b, use_right)
    mapped, norm = total
    norm = jnp.sum(norm, axis=1, keepdims=True)
    spread(qg, mapped, s_q, r_q)
    pass_on(qg, s_q, r_q)
    total = [zero]

    def use_mapped(n):
        total[0] = total[0] + whole(bg, n) * whole(qg, n)

    collect(qg, r_q, use_mapped)
    step = norm / jnp.sum(total[0], axis=1, keepdims=True)

    def residuals(n, total):
        res = whole(bg, n) - step * whole(qg, n)
        return total + res * res

    beta = jnp.sum(lax.fori_loop(0, 16, residuals, zero), axis=1, keepdims=True) / norm

    def directions(n, total):
        b = whole(bg, n)
        high, low = halves(b - step * whole(qg, n) + beta * b)
        pg[n, 0:80] = high
        pg[n, 80:160] = low
        return total + op_term(pg, n)

    product = lax.fori_loop(0, 16, directions, zero)
    product = whole(pg, 0) * product
    product = jnp.concatenate([product, jnp.zeros((48, 256), F32)], axis=0)
    tiny[0] = dot(jnp.ones((8, 256), F32), product, NT, lax.Precision.HIGHEST)
    for i, j in others:
        at = (4 - i) % 4 * 4 + (4 - j) % 4
        send(tiny.at[0], tiny.at[at], s_t.at[at], r_t.at[at], plane_peer(i, j))

    first = 5 * (4 * y + x)
    line = lax.broadcasted_iota(jnp.int32, (16, 80), 0)
    column = lax.broadcasted_iota(jnp.int32, (16, 80), 1)
    pick = jnp.where((line < 5) & (column == line + first), 1.0, 0.0).astype(BF16)

    def picked(buf, n):
        return (dot(pick, buf[n, 0:80]) + dot(pick, buf[n, 80:160]))[0:8]

    bs = [picked(bg, n) for n in range(16)]
    ms = [picked(qg, n) for n in range(16)]

    def row_sum(parts):
        total = parts[0]
        for part in parts[1:]:
            total = total + part
        return jnp.sum(total, axis=1, keepdims=True)

    norm5 = row_sum([b * b for b in bs])
    step5 = norm5 / row_sum([b * m for b, m in zip(bs, ms)])
    rs = [b - step5 * m for b, m in zip(bs, ms)]
    next5 = row_sum([v * v for v in rs])
    ps = [v + next5 / norm5 * b for v, b in zip(rs, bs)]

    for i, j in reversed(others):
        at = 4 * i + j
        arrived(tiny.at[at], r_t.at[at])
    curv = tiny[0]
    for n in range(1, 16):
        curv = curv + tiny[n]
    line = lax.broadcasted_iota(jnp.int32, (8, 128), 0)
    column = lax.broadcasted_iota(jnp.int32, (8, 128), 1)
    curv = jnp.sum(jnp.where(column == line + first, curv, 0.0), axis=1, keepdims=True)
    step2 = next5 / curv
    for i in range(4):
        for j in range(4):
            n = 4 * i + j
            value = step5 * bs[n] + step2 * ps[n]
            col = pl.multiple_of(block_row(i, j) * 256, 256)
            out_ref[:, pl.ds(col, 256)] = value[0:5]
    for copy in sent:
        copy.wait_send()


def local(silo_grams, silo_weights):
    dma = pltpu.SemaphoreType.DMA
    scratch = [
        pltpu.VMEM((2, 256, 640), BF16),
        pltpu.VMEM((16, 2, 256, 256), F32),
        pltpu.VMEM((16, 512, 256), BF16),
        pltpu.VMEM((16, 512, 256), BF16),
        pltpu.VMEM((2, 4, 80, 512), BF16),
        pltpu.VMEM((16, 4, 80, 256), F32),
        pltpu.VMEM((16, 4, 80, 256), F32),
        pltpu.VMEM((16, 4, 80, 256), F32),
        pltpu.VMEM((2, 2, 4, 80, 256), F32),
        pltpu.VMEM((2, 4, 4, 80, 256), F32),
        pltpu.VMEM((3, 4, 80, 256), F32),
        pltpu.VMEM((3, 80, 256), F32),
        pltpu.VMEM((16, 256, 256), F32),
        pltpu.VMEM((8, 256, 256), F32),
        pltpu.VMEM((2, 256, 256), F32),
        pltpu.VMEM((2, 2, 256, 256), F32),
        pltpu.VMEM((16, 2, 256, 256), BF16),
        pltpu.VMEM((16, 160, 256), BF16),
        pltpu.VMEM((16, 160, 256), BF16),
        pltpu.VMEM((16, 160, 256), BF16),
        pltpu.VMEM((16, 8, 128), F32),
    ]
    counts = [1, 16, 5, 5, 8, 8, 6, 6, 3, 3, 1, 1, 6, 6, 4, 4, 5, 5, 16, 16, 16, 16, 16, 16]
    scratch += [dma((n,)) for n in counts]
    return pl.pallas_call(
        kernel,
        out_shape=jax.ShapeDtypeStruct((5, 4096), F32),
        in_specs=[pl.BlockSpec(memory_space=pl.ANY)] * 2,
        out_specs=pl.BlockSpec(memory_space=pltpu.VMEM),
        scratch_shapes=scratch,
        compiler_params=pltpu.CompilerParams(collective_id=0, has_side_effects=True, vmem_limit_bytes=62 << 20),
        cost_estimate=pl.CostEstimate(flops=6_500_000_000, bytes_accessed=9_200_000, transcendentals=0),
    )(silo_grams, silo_weights)


def solution(mesh):
    torus = Mesh(mesh.devices.reshape(4, 2, 4, 4), AXES)
    silo, row = ("z", "core"), ("y", "x")
    in_specs = (P(silo, row, None), P(silo, row, None))
    out_specs = P(silo + row, None)
    return jax.shard_map(local, mesh=torus, in_specs=in_specs, out_specs=out_specs, check_vma=False)
```

```python
import jax
import jax.numpy as jnp
from jax import lax
from jax.experimental import pallas as pl
from jax.experimental.pallas import tpu as pltpu
from jax.sharding import Mesh
from jax.sharding import PartitionSpec as P

F32, BF16 = jnp.float32, jnp.bfloat16
MESH = pl.DeviceIdType.MESH
AXES = ("z", "core", "y", "x")
NT = (((1,), (1,)), ((), ()))
NN = (((1,), (0,)), ((), ()))
NEAR = (1, 3, 2)
FAR = (2, 1, 3, 0)


def dot(a, b, dims=NN, precision=None):
    return lax.dot_general(a, b, dims, precision=precision, preferred_element_type=F32)


def halves(value):
    high = value.astype(BF16)
    return high, (value - high.astype(F32)).astype(BF16)


def kernel(
    g_hbm, w_hbm, out_ref,
    w_raw, g, gh, gl, wt, p, q, r, far, near, second, third,
    ap, a_sib, a_far, a_near, a_op, bg, qg, pg, five_out, five_in, tiny,
    w_sem, load_sem, s_sib, r_sib, s_one, r_one, s_two, r_two, s_z, r_z,
    s_asib, r_asib, s_ars, r_ars, s_aag, r_aag, s_afw, r_afw,
    s_b, r_b, s_q, r_q, s_f, r_f, s_t, r_t,
):
    z, k, y, x = (lax.axis_index(a) for a in AXES)

    def dxy(i, j):
        return (1 - k) * i + k * j, (1 - k) * j + k * i

    def block_row(i, j):
        dx, dy = dxy(i, j)
        return lax.rem(y + dy, 4) * 4 + lax.rem(x + dx, 4)

    def canon(i, j):
        dx, dy = dxy(i, j)
        return dx * 4 + dy

    def plane_peer(i, j):
        dx, dy = dxy(i, j)
        return (z, k, lax.rem(y + dy, 4), lax.rem(x + dx, 4))

    def z_peer(d):
        return (lax.rem(z + d, 4), k, y, x)

    sibling = (z, 1 - k, y, x)

    def remote(src, dst, ssem, rsem, device):
        return pltpu.make_async_remote_copy(src, dst, ssem, rsem, device_id=device, device_id_type=MESH)

    sent = []

    def send(*args):
        copy = remote(*args)
        copy.start()
        sent.append(copy)

    def arrived(dst, rsem):
        remote(dst, dst, s_sib.at[0], rsem, sibling).wait_recv()

    weights = pltpu.make_async_copy(w_hbm, w_raw, w_sem.at[0])
    weights.start()

    def load(i, j):
        col = pl.multiple_of(block_row(i, j) * 256, 256)
        return pltpu.make_async_copy(g_hbm.at[:, :, pl.ds(col, 256)], g.at[4 * i + j], load_sem.at[4 * i + j])

    early = [(0, 2), (1, 2), (2, 0), (2, 1), (2, 2), (3, 2), (2, 3)]
    late = [(i, j) for j in (1, 3) for i in (0, 1, 3)] + [(1, 0), (3, 0), (0, 0)]
    for i, j in early + late:
        load(i, j).start()

    barrier = pltpu.get_barrier_semaphore()
    others = [(i, j) for i in FAR for j in FAR if i or j]
    for i, j in others:
        pl.semaphore_signal(barrier, 1, device_id=plane_peer(i, j), device_id_type=MESH)
    for d in NEAR:
        pl.semaphore_signal(barrier, 1, device_id=z_peer(d), device_id_type=MESH)
    pl.semaphore_signal(barrier, 1, device_id=sibling, device_id_type=MESH)

    weights.wait()
    flipped = w_raw[...].reshape(512, 640).astype(F32).T.astype(BF16)
    for s in range(8):
        wt[s % 2, lax.rem(s // 2 + 4 - z, 4)] = flipped[s * 80 : (s + 1) * 80]

    def add_silos(i, j):
        load(i, j).wait()
        ap[canon(i, j)] = g[4 * i + j, 0] + g[4 * i + j, 1]

    def split(i, j):
        high, low = halves(g[4 * i + j])
        gh[4 * i + j] = high.reshape(512, 256)
        gl[4 * i + j] = low.reshape(512, 256)

    def tile(core, slot):
        w = wt[core].reshape(320, 512)
        return (dot(w, gh[slot]) + dot(w, gl[slot])).reshape(4, 80, 256)

    def loop(count, step):
        def body(n, carry):
            step(n)
            return carry

        if count == 2:
            step(0)
            step(1)
        else:
            lax.fori_loop(0, count, body, 0)

    def for_sibling(m, lo, count, sem):
        def step(n):
            q[4 * m + lo + n] = tile(1 - k, 4 * (lo + n) + m)

        loop(count, step)
        rows = pl.ds(4 * m + lo, count)
        send(q.at[rows], r.at[rows], s_sib.at[sem], r_sib.at[sem], sibling)

    def for_self(m, lo, count):
        def step(n):
            p[4 * m + lo + n] = tile(k, 4 * m + lo + n)

        loop(count, step)

    def add_sibling(m, lo, count, sem):
        rows = pl.ds(4 * m + lo, count)
        arrived(r.at[rows], r_sib.at[sem])

        def step(n):
            p[4 * m + lo + n] += r[4 * m + lo + n]

        loop(count, step)

    up, down = plane_peer(1, 0), plane_peer(3, 0)

    def prepare(*blocks):
        for block in blocks:
            add_silos(*block)
            split(*block)

    prepare(early[0], early[1])
    pl.semaphore_wait(barrier, 19)
    for_sibling(2, 0, 2, 0)
    prepare(early[2], early[3])
    for_self(2, 0, 2)
    prepare(early[4], early[5])
    for_sibling(2, 2, 2, 1)
    add_sibling(2, 0, 2, 0)
    send(p.at[pl.ds(8, 2)], far.at[0], s_one.at[0], r_one.at[0], up)
    prepare(early[6])
    for_self(2, 2, 2)

    for block in late:
        add_silos(*block)
    mine, theirs = pl.ds(8 * k, 8), pl.ds(8 * (1 - k), 8)
    send(ap.at[theirs], a_sib, s_asib.at[0], r_asib.at[0], sibling)
    add_sibling(2, 2, 2, 1)
    send(p.at[pl.ds(10, 2)], far.at[1], s_one.at[1], r_one.at[1], down)
    for block in late[:3]:
        split(*block)
    for_sibling(1, 0, 4, 2)
    arrived(a_sib, r_asib.at[0])

    def add_op(n):
        a_sib[n] += ap[8 * k + n]

    loop(8, add_op)

    def quarter(d, n):
        return 2 * lax.rem(z + d, 4) + n

    z_up, z_down = z_peer(1), z_peer(3)
    send(a_sib.at[quarter(2, 0)], a_far.at[0], s_ars.at[0], r_ars.at[0], z_up)
    send(a_sib.at[quarter(2, 1)], a_far.at[1], s_ars.at[1], r_ars.at[1], z_down)
    send(a_sib.at[quarter(1, 1)], a_near.at[0, 1], s_ars.at[2], r_ars.at[2], z_up)
    send(a_sib.at[quarter(3, 0)], a_near.at[1, 0], s_ars.at[3], r_ars.at[3], z_down)

    for block in late[3:]:
        split(*block)
    for_self(1, 0, 4)
    for_sibling(3, 0, 4, 3)
    add_sibling(1, 0, 4, 2)
    send(p.at[pl.ds(6, 2)], near.at[0, pl.ds(2, 2)], s_one.at[2], r_one.at[2], up)
    for_self(3, 0, 4)
    add_sibling(3, 0, 4, 3)
    send(p.at[pl.ds(12, 2)], near.at[1, pl.ds(0, 2)], s_one.at[3], r_one.at[3], down)
    for_sibling(0, 0, 4, 4)
    for_self(0, 0, 4)
    add_sibling(0, 0, 4, 4)

    arrived(far.at[0], r_one.at[0])
    for n in (1, 0):
        p[4 + n] += far[0, n]
        send(p.at[4 + n], near.at[0, n], s_one.at[4 + n], r_one.at[4 + n], up)
    arrived(far.at[1], r_one.at[1])
    for n in range(2):
        p[14 + n] += far[1, n]
        send(p.at[14 + n], near.at[1, 2 + n], s_one.at[6 + n], r_one.at[6 + n], down)

    arrived(a_far.at[0], r_ars.at[0])
    a_sib[quarter(1, 0)] += a_far[0]
    send(a_sib.at[quarter(1, 0)], a_near.at[0, 0], s_ars.at[4], r_ars.at[4], z_up)
    arrived(a_far.at[1], r_ars.at[1])
    a_sib[quarter(3, 1)] += a_far[1]
    send(a_sib.at[quarter(3, 1)], a_near.at[1, 1], s_ars.at[5], r_ars.at[5], z_down)

    def second_axis(d):
        send(p.at[d, pl.ds(1, 3)], second.at[3 - d, pl.ds(1, 3)], s_two.at[3 - d], r_two.at[3 - d], plane_peer(0, d))
        send(p.at[d, 0], second.at[3 - d, 0], s_two.at[6 - d], r_two.at[6 - d], plane_peer(0, d))

    def whole_sum(n):
        p[n] += near[0, n] + near[1, n]

    arrived(near.at[0, pl.ds(2, 2)], r_one.at[2])
    arrived(near.at[1, pl.ds(0, 2)], r_one.at[3])
    arrived(near.at[0, 1], r_one.at[5])
    whole_sum(1)
    second_axis(1)
    arrived(near.at[1, 2], r_one.at[6])
    whole_sum(2)
    second_axis(2)

    arrived(a_near.at[0, 1], r_ars.at[2])
    arrived(a_near.at[1, 0], r_ars.at[3])
    arrived(a_near.at[0, 0], r_ars.at[4])
    arrived(a_near.at[1, 1], r_ars.at[5])

    def pass_op(at, ssem, rsem, device):
        send(a_op.at[at], a_op.at[at], ssem, rsem, device)

    own = 8 * k + quarter(0, 0)
    for n in range(2):
        high, low = halves(a_sib[quarter(0, n)] + a_near[0, n] + a_near[1, n])
        a_op[own + n, 0] = high
        a_op[own + n, 1] = low
    pass_op(own, s_aag.at[0], r_aag.at[0], z_up)
    pass_op(own + 1, s_aag.at[1], r_aag.at[1], z_down)
    pass_op(own + 1, s_aag.at[2], r_aag.at[2], z_up)
    pass_op(own, s_aag.at[3], r_aag.at[3], z_down)

    arrived(near.at[1, 3], r_one.at[7])
    whole_sum(3)
    second_axis(3)
    arrived(near.at[0, 0], r_one.at[4])
    whole_sum(0)

    for d in NEAR:
        arrived(second.at[3 - d, pl.ds(1, 3)], r_two.at[3 - d])
    for d in NEAR:
        p[0, d] += second[0, d] + second[1, d] + second[2, d]
        send(p.at[0, d], third.at[3 - d], s_z.at[3 - d], r_z.at[3 - d], z_peer(d))
    for d in NEAR:
        arrived(second.at[3 - d, 0], r_two.at[6 - d])
    right = p[0, 0] + second[0, 0] + second[1, 0] + second[2, 0]

    below, above, across = (8 * k + quarter(d, 0) for d in (3, 1, 2))
    arrived(a_op.at[below], r_aag.at[0])
    pass_op(below, s_aag.at[4], r_aag.at[4], z_up)
    arrived(a_op.at[above + 1], r_aag.at[1])
    pass_op(above + 1, s_aag.at[5], r_aag.at[5], z_down)
    for n in range(2):
        pass_op(own + n, s_afw.at[n], r_afw.at[n], sibling)

    for d in NEAR:
        arrived(third.at[3 - d], r_z.at[3 - d])
    right = right + third[0] + third[1] + third[2]

    def spread(buf, ss, rs):
        for d in NEAR:
            send(buf.at[0], buf.at[16 - 4 * d], ss.at[16 - 4 * d], rs.at[16 - 4 * d], plane_peer(d, 0))
        for d in NEAR:
            send(buf.at[0], buf.at[4 - d], ss.at[4 - d], rs.at[4 - d], plane_peer(0, d))

    def pass_on(buf, ss, rs):
        for i in NEAR:
            arrived(buf.at[4 * i], rs.at[4 * i])
            for d in NEAR:
                at = 4 * i + 4 - d
                send(buf.at[4 * i], buf.at[at], ss.at[at], rs.at[at], plane_peer(0, d))

    def collect(buf, rs, use):
        for i in range(4):
            use(4 * i)
        for i in (0, 1, 3, 2):
            for j in NEAR:
                at = 4 * i + j
                arrived(buf.at[at], rs.at[at])
                use(at)

    def right_block(n):
        return bg[n, 0:80].astype(F32) + bg[n, 80:160].astype(F32)

    high, low = halves(right)
    bg[0, 0:80] = high
    bg[0, 80:160] = low
    spread(bg, s_b, r_b)
    pass_on(bg, s_b, r_b)

    for at, n in ((below, 0), (above + 1, 1), (below + 1, 2), (above, 3), (across, 4), (across + 1, 5)):
        if n > 1:
            arrived(a_op.at[at], r_aag.at[n])
        pass_op(at, s_afw.at[2 + n], r_afw.at[2 + n], sibling)
    other = 8 * (1 - 2 * k)
    for n, at in enumerate((own, own + 1, below, above + 1, below + 1, above, across, across + 1)):
        arrived(a_op.at[at + other], r_afw.at[n])

    zero = jnp.zeros((80, 256), F32)
    total = [zero, zero]

    def use_right(n):
        at = canon(n // 4, n % 4)
        wide = dot(bg[n], a_op[at, 0], NT)
        total[0] = total[0] + wide[0:80] + wide[80:160] + dot(bg[n, 0:80], a_op[at, 1], NT)
        b = right_block(n)
        total[1] = total[1] + b * b

    collect(bg, r_b, use_right)
    mapped, norm = total
    norm = jnp.sum(norm, axis=1, keepdims=True)

    high, low = halves(mapped)
    qg[0] = high
    spread(qg, s_q, r_q)
    pass_on(qg, s_q, r_q)

    line = lax.broadcasted_iota(jnp.int32, (128, 80), 0)
    column = lax.broadcasted_iota(jnp.int32, (128, 80), 1)
    slot, line = lax.shift_right_logical(line, 3), line & 7
    dx, dy = dxy(lax.shift_right_logical(slot, 2), slot & 3)
    row = ((y + dy) & 3) * 4 + ((x + dx) & 3)
    pick = jnp.where((line < 5) & (column == line + 5 * row), 1.0, 0.0).astype(BF16)
    five_out[...] = (dot(pick, high) + dot(pick, low)).reshape(16, 8, 256)
    for i, j in others:
        at = (4 - i) % 4 * 4 + (4 - j) % 4
        send(five_out.at[4 * i + j], five_in.at[at], s_f.at[at], r_f.at[at], plane_peer(i, j))

    first = 5 * (4 * y + x)
    line = lax.broadcasted_iota(jnp.int32, (16, 80), 0)
    column = lax.broadcasted_iota(jnp.int32, (16, 80), 1)
    pick = jnp.where((line < 5) & (column == line + first), 1.0, 0.0).astype(BF16)
    bs = [(dot(pick, bg[n, 0:80]) + dot(pick, bg[n, 80:160]))[0:8] for n in range(16)]

    total = [zero]

    def use_mapped(n):
        total[0] = total[0] + right_block(n) * qg[n].astype(F32)

    collect(qg, r_q, use_mapped)
    step = norm / jnp.sum(total[0], axis=1, keepdims=True)

    def residuals(n, total):
        res = right_block(n) - step * qg[n].astype(F32)
        return total + res * res

    beta = jnp.sum(lax.fori_loop(0, 16, residuals, zero), axis=1, keepdims=True) / norm

    def directions(n, total):
        b = right_block(n)
        close = (b - step * qg[n].astype(F32) + beta * b).astype(BF16)
        at = canon(n // 4, n % 4)

        @pl.when(n == 0)
        def _():
            pg[...] = close

        return total + dot(close, a_op[at, 0], NT) + dot(close, a_op[at, 1], NT)

    image = lax.fori_loop(0, 16, directions, zero)
    products = [right_block(0) * image, mapped * image, pg[...].astype(F32) * image, jnp.zeros((16, 256), F32)]
    tiny[0] = dot(jnp.ones((8, 256), F32), jnp.concatenate(products, axis=0), NT, lax.Precision.HIGHEST)
    for i, j in others:
        at = (4 - i) % 4 * 4 + (4 - j) % 4
        send(tiny.at[0], tiny.at[at], s_t.at[at], r_t.at[at], plane_peer(i, j))

    for i, j in reversed(others):
        at = 4 * i + j
        arrived(five_in.at[at], r_f.at[at])
    ms = [five_out[0]] + [five_in[n] for n in range(1, 16)]

    def row_sum(parts):
        total = parts[0]
        for part in parts[1:]:
            total = total + part
        return jnp.sum(total, axis=1, keepdims=True)

    norm5 = row_sum([b * b for b in bs])
    step5 = norm5 / row_sum([b * m for b, m in zip(bs, ms)])
    rs = [b - step5 * m for b, m in zip(bs, ms)]
    next5 = row_sum([v * v for v in rs])
    beta5 = next5 / norm5
    ps = [v + beta5 * b for v, b in zip(rs, bs)]

    for i, j in reversed(others):
        at = 4 * i + j
        arrived(tiny.at[at], r_t.at[at])
    sums = tiny[0]
    for n in range(1, 16):
        sums = sums + tiny[n]
    line = lax.broadcasted_iota(jnp.int32, (8, 256), 0)
    column = lax.broadcasted_iota(jnp.int32, (8, 256), 1)

    def five(start):
        return jnp.sum(jnp.where(column == line + (first + start), sums, 0.0), axis=1, keepdims=True)

    curv = 2.0 * ((1.0 + beta5) * five(0) - step5 * five(80)) - five(160)
    step2 = next5 / curv
    for i in range(4):
        for j in range(4):
            n = 4 * i + j
            value = step5 * bs[n] + step2 * ps[n]
            col = pl.multiple_of(block_row(i, j) * 256, 256)
            out_ref[:, pl.ds(col, 256)] = value[0:5]
    for copy in sent:
        copy.wait_send()


def local(silo_grams, silo_weights):
    dma = pltpu.SemaphoreType.DMA
    scratch = [
        pltpu.VMEM((2, 256, 640), BF16),
        pltpu.VMEM((16, 2, 256, 256), F32),
        pltpu.VMEM((16, 512, 256), BF16),
        pltpu.VMEM((16, 512, 256), BF16),
        pltpu.VMEM((2, 4, 80, 512), BF16),
        pltpu.VMEM((16, 4, 80, 256), F32),
        pltpu.VMEM((16, 4, 80, 256), F32),
        pltpu.VMEM((16, 4, 80, 256), F32),
        pltpu.VMEM((2, 2, 4, 80, 256), F32),
        pltpu.VMEM((2, 4, 4, 80, 256), F32),
        pltpu.VMEM((3, 4, 80, 256), F32),
        pltpu.VMEM((3, 80, 256), F32),
        pltpu.VMEM((16, 256, 256), F32),
        pltpu.VMEM((8, 256, 256), F32),
        pltpu.VMEM((2, 256, 256), F32),
        pltpu.VMEM((2, 2, 256, 256), F32),
        pltpu.VMEM((16, 2, 256, 256), BF16),
        pltpu.VMEM((16, 160, 256), BF16),
        pltpu.VMEM((16, 80, 256), BF16),
        pltpu.VMEM((80, 256), BF16),
        pltpu.VMEM((16, 8, 256), F32),
        pltpu.VMEM((16, 8, 256), F32),
        pltpu.VMEM((16, 8, 256), F32),
    ]
    counts = [1, 16, 5, 5, 8, 8, 6, 6, 3, 3, 1, 1, 6, 6, 6, 6, 8, 8, 16, 16, 16, 16, 16, 16, 16, 16]
    scratch += [dma((n,)) for n in counts]
    return pl.pallas_call(
        kernel,
        out_shape=jax.ShapeDtypeStruct((5, 4096), F32),
        in_specs=[pl.BlockSpec(memory_space=pl.ANY)] * 2,
        out_specs=pl.BlockSpec(memory_space=pltpu.VMEM),
        scratch_shapes=scratch,
        compiler_params=pltpu.CompilerParams(collective_id=0, has_side_effects=True, vmem_limit_bytes=62 << 20),
        cost_estimate=pl.CostEstimate(flops=6_500_000_000, bytes_accessed=9_200_000, transcendentals=0),
    )(silo_grams, silo_weights)


def solution(mesh):
    torus = Mesh(mesh.devices.reshape(4, 2, 4, 4), AXES)
    silo, row = ("z", "core"), ("y", "x")
    in_specs = (P(silo, row, None), P(silo, row, None))
    out_specs = P(silo + row, None)
    return jax.shard_map(local, mesh=torus, in_specs=in_specs, out_specs=out_specs, check_vma=False)
```

```python
import jax
import jax.numpy as jnp
from jax import lax
from jax.experimental import pallas as pl
from jax.experimental.pallas import tpu as pltpu
from jax.sharding import Mesh
from jax.sharding import PartitionSpec as P

F32, BF16 = jnp.float32, jnp.bfloat16
MESH = pl.DeviceIdType.MESH
AXES = ("z", "core", "y", "x")
NT = (((1,), (1,)), ((), ()))
NN = (((1,), (0,)), ((), ()))
NEAR = (1, 3, 2)
FAR = (2, 1, 3, 0)


def dot(a, b, dims=NN, precision=None):
    return lax.dot_general(a, b, dims, precision=precision, preferred_element_type=F32)


def halves(value):
    high = value.astype(BF16)
    return high, (value - high.astype(F32)).astype(BF16)


def kernel(
    g_hbm, w_hbm, out_ref,
    w_raw, g, wt, p, q, r, far, near, second, third,
    ap, a_sib, a_far, a_near, a_op, bg, qg, five_out, five_in, tiny,
    w_sem, load_sem, s_sib, r_sib, s_one, r_one, s_two, r_two, s_z, r_z,
    s_asib, r_asib, s_ars, r_ars, s_aag, r_aag, s_afw, r_afw,
    s_b, r_b, s_q, r_q, s_f, r_f, s_t, r_t,
):
    z, k, y, x = (lax.axis_index(a) for a in AXES)

    def dxy(i, j):
        return (1 - k) * i + k * j, (1 - k) * j + k * i

    def block_row(i, j):
        dx, dy = dxy(i, j)
        return lax.rem(y + dy, 4) * 4 + lax.rem(x + dx, 4)

    def canon(i, j):
        dx, dy = dxy(i, j)
        return dx * 4 + dy

    def plane_peer(i, j):
        dx, dy = dxy(i, j)
        return (z, k, lax.rem(y + dy, 4), lax.rem(x + dx, 4))

    def z_peer(d):
        return (lax.rem(z + d, 4), k, y, x)

    sibling = (z, 1 - k, y, x)

    def remote(src, dst, ssem, rsem, device):
        return pltpu.make_async_remote_copy(src, dst, ssem, rsem, device_id=device, device_id_type=MESH)

    sent = []

    def send(*args):
        copy = remote(*args)
        copy.start()
        sent.append(copy)

    def arrived(dst, rsem):
        remote(dst, dst, s_sib.at[0], rsem, sibling).wait_recv()

    weights = pltpu.make_async_copy(w_hbm, w_raw, w_sem.at[0])
    weights.start()

    def load(i, j):
        col = pl.multiple_of(block_row(i, j) * 256, 256)
        return pltpu.make_async_copy(g_hbm.at[:, :, pl.ds(col, 256)], g.at[4 * i + j], load_sem.at[4 * i + j])

    blocks = [(2, 2), (1, 2), (2, 1), (2, 0), (0, 2), (2, 3), (3, 2), (1, 3), (3, 1), (3, 0), (0, 3)]
    blocks += [(1, 1), (1, 0), (0, 1), (3, 3), (0, 0)]
    for i, j in blocks:
        load(i, j).start()

    barrier = pltpu.get_barrier_semaphore()
    others = [(i, j) for i in FAR for j in FAR if i or j]
    for i, j in others:
        pl.semaphore_signal(barrier, 1, device_id=plane_peer(i, j), device_id_type=MESH)
    for d in NEAR:
        pl.semaphore_signal(barrier, 1, device_id=z_peer(d), device_id_type=MESH)
    pl.semaphore_signal(barrier, 1, device_id=sibling, device_id_type=MESH)

    weights.wait()
    flipped = w_raw[...].reshape(512, 640).astype(F32).T.astype(BF16)
    for s in range(8):
        wt[lax.rem(s + k, 2), lax.rem(s // 2 + 4 - z, 4)] = flipped[s * 80 : (s + 1) * 80]

    summed = []

    def add_silos(count):
        for i, j in blocks[len(summed) : count]:
            load(i, j).wait()
            ap[canon(i, j)] = g[4 * i + j, 0] + g[4 * i + j, 1]
            summed.append((i, j))

    def tiles(lo, hi):
        add_silos(hi)
        for i, j in blocks[lo:hi]:
            high, low = halves(g[4 * i + j])
            w = wt[...].reshape(640, 512)
            both = dot(w, high.reshape(512, 256)) + dot(w, low.reshape(512, 256))
            p[4 * i + j] = both[:320].reshape(4, 80, 256)
            q[4 * j + i] = both[320:].reshape(4, 80, 256)

    def to_sibling(lo, count, sem):
        rows = pl.ds(lo, count)
        send(q.at[rows], r.at[rows], s_sib.at[sem], r_sib.at[sem], sibling)

    def add_sibling(lo, count, sem):
        rows = pl.ds(lo, count)
        arrived(r.at[rows], r_sib.at[sem])
        for n in range(lo, lo + count):
            p[n] += r[n]

    def quarter(d, n):
        return 2 * lax.rem(z + d, 4) + n

    up, down = plane_peer(1, 0), plane_peer(3, 0)
    z_up, z_down = z_peer(1), z_peer(3)

    tiles(0, 3)
    pl.semaphore_wait(barrier, 19)
    to_sibling(9, 2, 0)
    tiles(3, 5)
    to_sibling(8, 1, 1)
    add_sibling(9, 2, 0)
    send(p.at[9], far.at[0, 1], s_one.at[0], r_one.at[0], up)
    send(p.at[10], far.at[1, 0], s_one.at[1], r_one.at[1], down)

    def op_to_sibling(d):
        rows = pl.ds(quarter(d, 0), 2)
        send(ap.at[pl.ds(8 * (1 - k) + quarter(d, 0), 2)], a_sib.at[rows], s_asib.at[d], r_asib.at[d], sibling)

    def op_from_sibling(d):
        arrived(a_sib.at[pl.ds(quarter(d, 0), 2)], r_asib.at[d])
        for n in range(2):
            a_sib[quarter(d, n)] += ap[8 * k + quarter(d, n)]

    add_silos(16)
    op_to_sibling(2)
    tiles(5, 7)
    to_sibling(11, 1, 2)
    add_sibling(8, 1, 1)
    send(p.at[8], far.at[0, 0], s_one.at[8], r_one.at[8], up)
    op_from_sibling(2)
    send(a_sib.at[quarter(2, 0)], a_far.at[0], s_ars.at[0], r_ars.at[0], z_up)
    send(a_sib.at[quarter(2, 1)], a_far.at[1], s_ars.at[1], r_ars.at[1], z_down)
    tiles(7, 9)
    add_sibling(11, 1, 2)
    send(p.at[11], far.at[1, 1], s_one.at[9], r_one.at[9], down)
    tiles(9, 11)
    to_sibling(6, 2, 3)
    to_sibling(12, 2, 4)
    op_to_sibling(1)
    op_to_sibling(3)
    tiles(11, 13)
    add_sibling(6, 2, 3)
    send(p.at[pl.ds(6, 2)], near.at[0, pl.ds(2, 2)], s_one.at[2], r_one.at[2], up)
    add_sibling(12, 2, 4)
    send(p.at[pl.ds(12, 2)], near.at[1, pl.ds(0, 2)], s_one.at[3], r_one.at[3], down)
    tiles(13, 15)
    to_sibling(4, 2, 5)
    to_sibling(14, 2, 6)
    op_from_sibling(1)
    send(a_sib.at[quarter(1, 1)], a_near.at[0, 1], s_ars.at[2], r_ars.at[2], z_up)
    op_from_sibling(3)
    send(a_sib.at[quarter(3, 0)], a_near.at[1, 0], s_ars.at[3], r_ars.at[3], z_down)
    tiles(15, 16)
    to_sibling(0, 4, 7)
    op_to_sibling(0)
    add_sibling(4, 2, 5)
    add_sibling(14, 2, 6)

    def relay_up(n, sem):
        arrived(far.at[0, n], r_one.at[sem])
        p[4 + n] += far[0, n]
        send(p.at[4 + n], near.at[0, n], s_one.at[4 + n], r_one.at[4 + n], up)

    def relay_down(n, sem):
        arrived(far.at[1, n], r_one.at[sem])
        p[14 + n] += far[1, n]
        send(p.at[14 + n], near.at[1, 2 + n], s_one.at[6 + n], r_one.at[6 + n], down)

    relay_up(1, 0)
    relay_down(0, 1)
    add_sibling(0, 4, 7)
    relay_up(0, 8)
    relay_down(1, 9)
    arrived(a_far.at[0], r_ars.at[0])
    a_sib[quarter(1, 0)] += a_far[0]
    send(a_sib.at[quarter(1, 0)], a_near.at[0, 0], s_ars.at[4], r_ars.at[4], z_up)
    arrived(a_far.at[1], r_ars.at[1])
    a_sib[quarter(3, 1)] += a_far[1]
    send(a_sib.at[quarter(3, 1)], a_near.at[1, 1], s_ars.at[5], r_ars.at[5], z_down)

    def second_axis(d):
        send(p.at[d, pl.ds(1, 3)], second.at[3 - d, pl.ds(1, 3)], s_two.at[3 - d], r_two.at[3 - d], plane_peer(0, d))
        send(p.at[d, 0], second.at[3 - d, 0], s_two.at[6 - d], r_two.at[6 - d], plane_peer(0, d))

    def whole_sum(n):
        p[n] += near[0, n] + near[1, n]

    arrived(near.at[0, pl.ds(2, 2)], r_one.at[2])
    arrived(near.at[1, pl.ds(0, 2)], r_one.at[3])
    arrived(near.at[0, 1], r_one.at[5])
    whole_sum(1)
    second_axis(1)
    arrived(near.at[1, 2], r_one.at[6])
    whole_sum(2)
    second_axis(2)

    arrived(a_near.at[0, 1], r_ars.at[2])
    arrived(a_near.at[1, 0], r_ars.at[3])
    arrived(a_near.at[0, 0], r_ars.at[4])
    arrived(a_near.at[1, 1], r_ars.at[5])

    def pass_op(at, ssem, rsem, device):
        send(a_op.at[at], a_op.at[at], ssem, rsem, device)

    op_from_sibling(0)
    own = 8 * k + quarter(0, 0)
    for n in range(2):
        high, low = halves(a_sib[quarter(0, n)] + a_near[0, n] + a_near[1, n])
        a_op[own + n, 0] = high
        a_op[own + n, 1] = low
    pass_op(own, s_aag.at[0], r_aag.at[0], z_up)
    pass_op(own + 1, s_aag.at[1], r_aag.at[1], z_down)
    pass_op(own + 1, s_aag.at[2], r_aag.at[2], z_up)
    pass_op(own, s_aag.at[3], r_aag.at[3], z_down)
    arrived(near.at[1, 3], r_one.at[7])
    whole_sum(3)
    second_axis(3)
    arrived(near.at[0, 0], r_one.at[4])
    whole_sum(0)

    for d in NEAR:
        arrived(second.at[3 - d, pl.ds(1, 3)], r_two.at[3 - d])
    for d in NEAR:
        p[0, d] += second[0, d] + second[1, d] + second[2, d]
        send(p.at[0, d], third.at[3 - d], s_z.at[3 - d], r_z.at[3 - d], z_peer(d))
    for d in NEAR:
        arrived(second.at[3 - d, 0], r_two.at[6 - d])
    right = p[0, 0] + second[0, 0] + second[1, 0] + second[2, 0]

    for d in NEAR:
        arrived(third.at[3 - d], r_z.at[3 - d])
    right = right + third[0] + third[1] + third[2]

    def spread(buf, ss, rs):
        for d in NEAR:
            send(buf.at[0], buf.at[16 - 4 * d], ss.at[16 - 4 * d], rs.at[16 - 4 * d], plane_peer(d, 0))
        for d in NEAR:
            send(buf.at[0], buf.at[4 - d], ss.at[4 - d], rs.at[4 - d], plane_peer(0, d))

    def pass_on(buf, ss, rs):
        for i in NEAR:
            arrived(buf.at[4 * i], rs.at[4 * i])
            for d in NEAR:
                at = 4 * i + 4 - d
                send(buf.at[4 * i], buf.at[at], ss.at[at], rs.at[at], plane_peer(0, d))

    def collect(buf, rs, use):
        for i in range(4):
            use(4 * i)
        for i in (0, 1, 3, 2):
            for j in NEAR:
                at = 4 * i + j
                arrived(buf.at[at], rs.at[at])
                use(at)

    def right_block(n):
        return bg[n, 0:80].astype(F32) + bg[n, 80:160].astype(F32)

    high, low = halves(right)
    bg[0, 0:80] = high
    bg[0, 80:160] = low
    spread(bg, s_b, r_b)

    below, above, across = (8 * k + quarter(d, 0) for d in (3, 1, 2))
    arrived(a_op.at[below], r_aag.at[0])
    pass_op(below, s_aag.at[4], r_aag.at[4], z_up)
    arrived(a_op.at[above + 1], r_aag.at[1])
    pass_op(above + 1, s_aag.at[5], r_aag.at[5], z_down)
    for n in range(2):
        pass_op(own + n, s_afw.at[n], r_afw.at[n], sibling)

    pass_on(bg, s_b, r_b)

    for at, n in ((below, 0), (above + 1, 1), (below + 1, 2), (above, 3), (across, 4), (across + 1, 5)):
        if n > 1:
            arrived(a_op.at[at], r_aag.at[n])
        pass_op(at, s_afw.at[2 + n], r_afw.at[2 + n], sibling)
    other = 8 * (1 - 2 * k)
    for n, at in enumerate((own, own + 1, below, above + 1, below + 1, above, across, across + 1)):
        arrived(a_op.at[at + other], r_afw.at[n])

    zero = jnp.zeros((80, 256), F32)
    total = [zero, zero]

    def use_right(n):
        at = canon(n // 4, n % 4)
        wide = dot(bg[n], a_op[at, 0], NT)
        total[0] = total[0] + wide[0:80] + wide[80:160] + dot(bg[n, 0:80], a_op[at, 1], NT)
        b = right_block(n)
        total[1] = total[1] + b * b

    collect(bg, r_b, use_right)
    mapped, norm = total
    norm = jnp.sum(norm, axis=1, keepdims=True)

    high, low = halves(mapped)
    qg[0] = high
    spread(qg, s_q, r_q)
    pass_on(qg, s_q, r_q)

    line = lax.broadcasted_iota(jnp.int32, (128, 80), 0)
    column = lax.broadcasted_iota(jnp.int32, (128, 80), 1)
    slot, line = lax.shift_right_logical(line, 3), line & 7
    dx, dy = dxy(lax.shift_right_logical(slot, 2), slot & 3)
    row = ((y + dy) & 3) * 4 + ((x + dx) & 3)
    pick = jnp.where((line < 5) & (column == line + 5 * row), 1.0, 0.0).astype(BF16)
    five_out[...] = (dot(pick, high) + dot(pick, low)).reshape(16, 8, 256)
    for i, j in others:
        at = (4 - i) % 4 * 4 + (4 - j) % 4
        send(five_out.at[4 * i + j], five_in.at[at], s_f.at[at], r_f.at[at], plane_peer(i, j))

    first = 5 * (4 * y + x)
    line = lax.broadcasted_iota(jnp.int32, (16, 80), 0)
    column = lax.broadcasted_iota(jnp.int32, (16, 80), 1)
    pick = jnp.where((line < 5) & (column == line + first), 1.0, 0.0).astype(BF16)
    bs = [(dot(pick, bg[n, 0:80]) + dot(pick, bg[n, 80:160]))[0:8] for n in range(16)]

    total = [zero, zero]

    def use_mapped(n):
        m = qg[n].astype(F32)
        total[0] = total[0] + right_block(n) * m
        total[1] = total[1] + m * m

    collect(qg, r_q, use_mapped)
    step = norm / jnp.sum(total[0], axis=1, keepdims=True)

    size = jnp.sum(total[1], axis=1, keepdims=True)
    beta = jnp.maximum(step * step * size / norm - 1.0, 0.0)

    image = zero
    for n in range(16):
        b = right_block(n)
        close = (b - step * qg[n].astype(F32) + beta * b).astype(BF16)
        at = canon(n // 4, n % 4)
        image = image + dot(close, a_op[at, 0], NT) + dot(close, a_op[at, 1], NT)
        if n == 0:
            mine = close.astype(F32)
    products = [right_block(0) * image, mapped * image, mine * image, jnp.zeros((16, 256), F32)]
    tiny[0] = dot(jnp.ones((8, 256), F32), jnp.concatenate(products, axis=0), NT, lax.Precision.HIGHEST)
    for i, j in others:
        at = (4 - i) % 4 * 4 + (4 - j) % 4
        send(tiny.at[0], tiny.at[at], s_t.at[at], r_t.at[at], plane_peer(i, j))

    for i, j in reversed(others):
        at = 4 * i + j
        arrived(five_in.at[at], r_f.at[at])
    ms = [five_out[0]] + [five_in[n] for n in range(1, 16)]

    def row_sum(parts):
        total = parts[0]
        for part in parts[1:]:
            total = total + part
        return jnp.sum(total, axis=1, keepdims=True)

    norm5 = row_sum([b * b for b in bs])
    step5 = norm5 / row_sum([b * m for b, m in zip(bs, ms)])
    rs = [b - step5 * m for b, m in zip(bs, ms)]
    next5 = row_sum([v * v for v in rs])
    beta5 = next5 / norm5
    ps = [v + beta5 * b for v, b in zip(rs, bs)]

    for i, j in reversed(others):
        at = 4 * i + j
        arrived(tiny.at[at], r_t.at[at])
    sums = tiny[0]
    for n in range(1, 16):
        sums = sums + tiny[n]
    line = lax.broadcasted_iota(jnp.int32, (8, 256), 0)
    column = lax.broadcasted_iota(jnp.int32, (8, 256), 1)

    def five(start):
        return jnp.sum(jnp.where(column == line + (first + start), sums, 0.0), axis=1, keepdims=True)

    curv = 2.0 * ((1.0 + beta5) * five(0) - step5 * five(80)) - five(160)
    step2 = next5 / curv
    for i in range(4):
        for j in range(4):
            n = 4 * i + j
            value = step5 * bs[n] + step2 * ps[n]
            col = pl.multiple_of(block_row(i, j) * 256, 256)
            out_ref[:, pl.ds(col, 256)] = value[0:5]
    for copy in sent:
        copy.wait_send()


def local(silo_grams, silo_weights):
    dma = pltpu.SemaphoreType.DMA
    scratch = [
        pltpu.VMEM((2, 256, 640), BF16),
        pltpu.VMEM((16, 2, 256, 256), F32),
        pltpu.VMEM((2, 4, 80, 512), BF16),
        pltpu.VMEM((16, 4, 80, 256), F32),
        pltpu.VMEM((16, 4, 80, 256), F32),
        pltpu.VMEM((16, 4, 80, 256), F32),
        pltpu.VMEM((2, 2, 4, 80, 256), F32),
        pltpu.VMEM((2, 4, 4, 80, 256), F32),
        pltpu.VMEM((3, 4, 80, 256), F32),
        pltpu.VMEM((3, 80, 256), F32),
        pltpu.VMEM((16, 256, 256), F32),
        pltpu.VMEM((8, 256, 256), F32),
        pltpu.VMEM((2, 256, 256), F32),
        pltpu.VMEM((2, 2, 256, 256), F32),
        pltpu.VMEM((16, 2, 256, 256), BF16),
        pltpu.VMEM((16, 160, 256), BF16),
        pltpu.VMEM((16, 80, 256), BF16),
        pltpu.VMEM((16, 8, 256), F32),
        pltpu.VMEM((16, 8, 256), F32),
        pltpu.VMEM((16, 8, 256), F32),
    ]
    counts = [1, 16, 8, 8, 10, 10, 6, 6, 3, 3, 4, 4, 6, 6, 6, 6, 8, 8, 16, 16, 16, 16, 16, 16, 16, 16]
    scratch += [dma((n,)) for n in counts]
    return pl.pallas_call(
        kernel,
        out_shape=jax.ShapeDtypeStruct((5, 4096), F32),
        in_specs=[pl.BlockSpec(memory_space=pl.ANY)] * 2,
        out_specs=pl.BlockSpec(memory_space=pltpu.VMEM),
        scratch_shapes=scratch,
        compiler_params=pltpu.CompilerParams(collective_id=0, has_side_effects=True, vmem_limit_bytes=62 << 20),
        cost_estimate=pl.CostEstimate(flops=6_500_000_000, bytes_accessed=9_200_000, transcendentals=0),
    )(silo_grams, silo_weights)


def solution(mesh):
    torus = Mesh(mesh.devices.reshape(4, 2, 4, 4), AXES)
    silo, row = ("z", "core"), ("y", "x")
    in_specs = (P(silo, row, None), P(silo, row, None))
    out_specs = P(silo + row, None)
    return jax.shard_map(local, mesh=torus, in_specs=in_specs, out_specs=out_specs, check_vma=False)
```

```python
import jax
import jax.numpy as jnp
from jax import lax
from jax.experimental import pallas as pl
from jax.experimental.pallas import tpu as pltpu
from jax.sharding import Mesh
from jax.sharding import PartitionSpec as P

F32, BF16 = jnp.float32, jnp.bfloat16
MESH = pl.DeviceIdType.MESH
AXES = ("z", "core", "y", "x")
NT = (((1,), (1,)), ((), ()))
NN = (((1,), (0,)), ((), ()))
NEAR = (1, 3, 2)
FAR = (2, 1, 3, 0)


def dot(a, b, dims=NN, precision=None):
    return lax.dot_general(a, b, dims, precision=precision, preferred_element_type=F32)


def halves(value):
    high = value.astype(BF16)
    return high, (value - high.astype(F32)).astype(BF16)


def kernel(
    g_hbm, w_hbm, out_ref,
    w_raw, g, wt, p, q, r, far, near, second, third,
    ap, a_sib, a_far, a_near, a_op, bg, bl, qg, acc, five_out, five_in, tiny,
    w_sem, load_sem, s_sib, r_sib, s_one, r_one, s_two, r_two, s_z, r_z,
    s_asib, r_asib, s_ars, r_ars, s_aag, r_aag, s_afw, r_afw,
    s_b, r_b, s_l, r_l, s_q, r_q, s_f, r_f, s_t, r_t,
):
    z, k, y, x = (lax.axis_index(a) for a in AXES)

    def dxy(i, j):
        return (1 - k) * i + k * j, (1 - k) * j + k * i

    def block_row(i, j):
        dx, dy = dxy(i, j)
        return lax.rem(y + dy, 4) * 4 + lax.rem(x + dx, 4)

    def canon(i, j):
        dx, dy = dxy(i, j)
        return dx * 4 + dy

    def plane_peer(i, j):
        dx, dy = dxy(i, j)
        return (z, k, lax.rem(y + dy, 4), lax.rem(x + dx, 4))

    def z_peer(d):
        return (lax.rem(z + d, 4), k, y, x)

    sibling = (z, 1 - k, y, x)

    def remote(src, dst, ssem, rsem, device):
        return pltpu.make_async_remote_copy(src, dst, ssem, rsem, device_id=device, device_id_type=MESH)

    sent = []

    def send(*args):
        copy = remote(*args)
        copy.start()
        sent.append(copy)

    def arrived(dst, rsem):
        remote(dst, dst, s_sib.at[0], rsem, sibling).wait_recv()

    weights = pltpu.make_async_copy(w_hbm, w_raw, w_sem.at[0])
    weights.start()

    def load(i, j):
        col = pl.multiple_of(block_row(i, j) * 256, 256)
        return pltpu.make_async_copy(g_hbm.at[:, :, pl.ds(col, 256)], g.at[4 * i + j], load_sem.at[4 * i + j])

    blocks = [(2, 2), (1, 2), (2, 1), (2, 0), (0, 2), (2, 3), (3, 2), (1, 3), (3, 1), (3, 0), (0, 3)]
    blocks += [(1, 1), (1, 0), (0, 1), (3, 3), (0, 0)]
    for i, j in blocks:
        load(i, j).start()

    barrier = pltpu.get_barrier_semaphore()
    others = [(i, j) for i in FAR for j in FAR if i or j]
    for i, j in others:
        pl.semaphore_signal(barrier, 1, device_id=plane_peer(i, j), device_id_type=MESH)
    for d in NEAR:
        pl.semaphore_signal(barrier, 1, device_id=z_peer(d), device_id_type=MESH)
    pl.semaphore_signal(barrier, 1, device_id=sibling, device_id_type=MESH)

    weights.wait()
    flipped = w_raw[...].reshape(512, 640).astype(F32).T.astype(BF16)
    for s in range(8):
        wt[lax.rem(s + k, 2), lax.rem(s // 2 + 4 - z, 4)] = flipped[s * 80 : (s + 1) * 80]

    summed = []

    def add_silos(count):
        for i, j in blocks[len(summed) : count]:
            load(i, j).wait()
            ap[canon(i, j)] = g[4 * i + j, 0] + g[4 * i + j, 1]
            summed.append((i, j))

    def tiles(lo, hi):
        add_silos(hi)
        for i, j in blocks[lo:hi]:
            high, low = halves(g[4 * i + j])
            w = wt[...].reshape(640, 512)
            both = dot(w, high.reshape(512, 256)) + dot(w, low.reshape(512, 256))
            p[4 * i + j] = both[:320].reshape(4, 80, 256)
            q[4 * j + i] = both[320:].reshape(4, 80, 256)

    def to_sibling(lo, count, sem):
        rows = pl.ds(lo, count)
        send(q.at[rows], r.at[rows], s_sib.at[sem], r_sib.at[sem], sibling)

    def add_sibling(lo, count, sem):
        rows = pl.ds(lo, count)
        arrived(r.at[rows], r_sib.at[sem])
        for n in range(lo, lo + count):
            p[n] += r[n]

    def quarter(d, n):
        return 2 * lax.rem(z + d, 4) + n

    up, down = plane_peer(1, 0), plane_peer(3, 0)
    z_up, z_down = z_peer(1), z_peer(3)

    tiles(0, 3)
    pl.semaphore_wait(barrier, 19)
    to_sibling(9, 2, 0)
    tiles(3, 5)
    to_sibling(8, 1, 1)
    add_sibling(9, 2, 0)
    send(p.at[9], far.at[0, 1], s_one.at[0], r_one.at[0], up)
    send(p.at[10], far.at[1, 0], s_one.at[1], r_one.at[1], down)

    def op_to_sibling(d):
        rows = pl.ds(quarter(d, 0), 2)
        send(ap.at[pl.ds(8 * (1 - k) + quarter(d, 0), 2)], a_sib.at[rows], s_asib.at[d], r_asib.at[d], sibling)

    def op_from_sibling(d):
        arrived(a_sib.at[pl.ds(quarter(d, 0), 2)], r_asib.at[d])
        for n in range(2):
            a_sib[quarter(d, n)] += ap[8 * k + quarter(d, n)]

    add_silos(16)
    op_to_sibling(2)
    tiles(5, 7)
    to_sibling(11, 1, 2)
    add_sibling(8, 1, 1)
    send(p.at[8], far.at[0, 0], s_one.at[8], r_one.at[8], up)
    op_from_sibling(2)
    send(a_sib.at[quarter(2, 0)], a_far.at[0], s_ars.at[0], r_ars.at[0], z_up)
    send(a_sib.at[quarter(2, 1)], a_far.at[1], s_ars.at[1], r_ars.at[1], z_down)
    tiles(7, 9)
    add_sibling(11, 1, 2)
    send(p.at[11], far.at[1, 1], s_one.at[9], r_one.at[9], down)
    tiles(9, 11)
    to_sibling(6, 2, 3)
    to_sibling(12, 2, 4)
    op_to_sibling(1)
    op_to_sibling(3)
    tiles(11, 13)
    add_sibling(6, 2, 3)
    send(p.at[pl.ds(6, 2)], near.at[0, pl.ds(2, 2)], s_one.at[2], r_one.at[2], up)
    add_sibling(12, 2, 4)
    send(p.at[pl.ds(12, 2)], near.at[1, pl.ds(0, 2)], s_one.at[3], r_one.at[3], down)
    tiles(13, 15)
    to_sibling(4, 2, 5)
    to_sibling(14, 2, 6)
    op_from_sibling(1)
    send(a_sib.at[quarter(1, 1)], a_near.at[0, 1], s_ars.at[2], r_ars.at[2], z_up)
    op_from_sibling(3)
    send(a_sib.at[quarter(3, 0)], a_near.at[1, 0], s_ars.at[3], r_ars.at[3], z_down)
    tiles(15, 16)
    to_sibling(0, 4, 7)
    op_to_sibling(0)
    add_sibling(4, 2, 5)
    add_sibling(14, 2, 6)

    def relay_up(n, sem):
        arrived(far.at[0, n], r_one.at[sem])
        p[4 + n] += far[0, n]
        send(p.at[4 + n], near.at[0, n], s_one.at[4 + n], r_one.at[4 + n], up)

    def relay_down(n, sem):
        arrived(far.at[1, n], r_one.at[sem])
        p[14 + n] += far[1, n]
        send(p.at[14 + n], near.at[1, 2 + n], s_one.at[6 + n], r_one.at[6 + n], down)

    relay_up(1, 0)
    relay_down(0, 1)
    add_sibling(0, 4, 7)
    relay_up(0, 8)
    relay_down(1, 9)
    arrived(a_far.at[0], r_ars.at[0])
    a_sib[quarter(1, 0)] += a_far[0]
    send(a_sib.at[quarter(1, 0)], a_near.at[0, 0], s_ars.at[4], r_ars.at[4], z_up)
    arrived(a_far.at[1], r_ars.at[1])
    a_sib[quarter(3, 1)] += a_far[1]
    send(a_sib.at[quarter(3, 1)], a_near.at[1, 1], s_ars.at[5], r_ars.at[5], z_down)

    def second_axis(d):
        send(p.at[d, pl.ds(1, 3)], second.at[3 - d, pl.ds(1, 3)], s_two.at[3 - d], r_two.at[3 - d], plane_peer(0, d))
        send(p.at[d, 0], second.at[3 - d, 0], s_two.at[6 - d], r_two.at[6 - d], plane_peer(0, d))

    def whole_sum(n):
        p[n] += near[0, n] + near[1, n]

    arrived(near.at[0, pl.ds(2, 2)], r_one.at[2])
    arrived(near.at[1, pl.ds(0, 2)], r_one.at[3])
    arrived(near.at[0, 1], r_one.at[5])
    whole_sum(1)
    second_axis(1)
    arrived(near.at[1, 2], r_one.at[6])
    whole_sum(2)
    second_axis(2)

    arrived(a_near.at[0, 1], r_ars.at[2])
    arrived(a_near.at[1, 0], r_ars.at[3])
    arrived(a_near.at[0, 0], r_ars.at[4])
    arrived(a_near.at[1, 1], r_ars.at[5])

    def pass_op(at, ssem, rsem, device):
        send(a_op.at[at], a_op.at[at], ssem, rsem, device)

    op_from_sibling(0)
    own = 8 * k + quarter(0, 0)
    for n in range(2):
        high, low = halves(a_sib[quarter(0, n)] + a_near[0, n] + a_near[1, n])
        a_op[own + n, 0] = high
        a_op[own + n, 1] = low
    pass_op(own, s_aag.at[0], r_aag.at[0], z_up)
    pass_op(own + 1, s_aag.at[1], r_aag.at[1], z_down)
    pass_op(own + 1, s_aag.at[2], r_aag.at[2], z_up)
    pass_op(own, s_aag.at[3], r_aag.at[3], z_down)
    arrived(near.at[1, 3], r_one.at[7])
    whole_sum(3)
    second_axis(3)
    arrived(near.at[0, 0], r_one.at[4])
    whole_sum(0)

    for d in NEAR:
        arrived(second.at[3 - d, pl.ds(1, 3)], r_two.at[3 - d])
    for d in NEAR:
        p[0, d] += second[0, d] + second[1, d] + second[2, d]
        send(p.at[0, d], third.at[3 - d], s_z.at[3 - d], r_z.at[3 - d], z_peer(d))
    for d in NEAR:
        arrived(second.at[3 - d, 0], r_two.at[6 - d])
    right = p[0, 0] + second[0, 0] + second[1, 0] + second[2, 0]

    for d in NEAR:
        arrived(third.at[3 - d], r_z.at[3 - d])
    right = right + third[0] + third[1] + third[2]

    def spread(buf, ss, rs):
        for d in NEAR:
            send(buf.at[0], buf.at[16 - 4 * d], ss.at[16 - 4 * d], rs.at[16 - 4 * d], plane_peer(d, 0))
        for d in NEAR:
            send(buf.at[0], buf.at[4 - d], ss.at[4 - d], rs.at[4 - d], plane_peer(0, d))

    def pass_on(buf, ss, rs):
        for i in NEAR:
            arrived(buf.at[4 * i], rs.at[4 * i])
            for d in NEAR:
                at = 4 * i + 4 - d
                send(buf.at[4 * i], buf.at[at], ss.at[at], rs.at[at], plane_peer(0, d))

    def collect(buf, rs, use):
        for i in range(4):
            use(4 * i)
        for i in (0, 1, 3, 2):
            for j in NEAR:
                at = 4 * i + j
                arrived(buf.at[at], rs.at[at])
                use(at)

    def right_block(n):
        return bg[n].astype(F32) + bl[n].astype(F32)

    high, low = halves(right)
    bg[0] = high
    bl[0] = low
    spread(bg, s_b, r_b)

    below, above, across = (8 * k + quarter(d, 0) for d in (3, 1, 2))
    arrived(a_op.at[below], r_aag.at[0])
    pass_op(below, s_aag.at[4], r_aag.at[4], z_up)
    arrived(a_op.at[above + 1], r_aag.at[1])
    pass_op(above + 1, s_aag.at[5], r_aag.at[5], z_down)
    for n in range(2):
        pass_op(own + n, s_afw.at[n], r_afw.at[n], sibling)

    pass_on(bg, s_b, r_b)
    spread(bl, s_l, r_l)

    for at, n in ((below, 0), (above + 1, 1), (below + 1, 2), (above, 3), (across, 4), (across + 1, 5)):
        if n > 1:
            arrived(a_op.at[at], r_aag.at[n])
        pass_op(at, s_afw.at[2 + n], r_afw.at[2 + n], sibling)
    other = 8 * (1 - 2 * k)
    for n, at in enumerate((own, own + 1, below, above + 1, below + 1, above, across, across + 1)):
        arrived(a_op.at[at + other], r_afw.at[n])

    zero = jnp.zeros((80, 256), F32)
    total = [zero]

    def use_high(n):
        at = canon(n // 4, n % 4)
        total[0] = total[0] + dot(bg[n], a_op[at, 0], NT) + dot(bg[n], a_op[at, 1], NT)

    collect(bg, r_b, use_high)
    acc[...] = total[0]
    qg[0] = total[0].astype(BF16)
    spread(qg, s_q, r_q)
    pass_on(bl, s_l, r_l)
    pass_on(qg, s_q, r_q)

    total = [zero]

    def use_low(n):
        total[0] = total[0] + dot(bl[n], a_op[canon(n // 4, n % 4), 0], NT)

    collect(bl, r_l, use_low)
    mapped = acc[...] + total[0]
    norm = zero
    for n in range(16):
        b = right_block(n)
        norm = norm + b * b
    norm = jnp.sum(norm, axis=1, keepdims=True)

    line = lax.broadcasted_iota(jnp.int32, (128, 80), 0)
    column = lax.broadcasted_iota(jnp.int32, (128, 80), 1)
    slot, line = lax.shift_right_logical(line, 3), line & 7
    dx, dy = dxy(lax.shift_right_logical(slot, 2), slot & 3)
    row = ((y + dy) & 3) * 4 + ((x + dx) & 3)
    pick = jnp.where((line < 5) & (column == line + 5 * row), 1.0, 0.0).astype(BF16)
    high, low = halves(mapped)
    five_out[...] = (dot(pick, high) + dot(pick, low)).reshape(16, 8, 256)
    for i, j in others:
        at = (4 - i) % 4 * 4 + (4 - j) % 4
        send(five_out.at[4 * i + j], five_in.at[at], s_f.at[at], r_f.at[at], plane_peer(i, j))

    first = 5 * (4 * y + x)
    line = lax.broadcasted_iota(jnp.int32, (16, 80), 0)
    column = lax.broadcasted_iota(jnp.int32, (16, 80), 1)
    pick = jnp.where((line < 5) & (column == line + first), 1.0, 0.0).astype(BF16)
    bs = [(dot(pick, bg[n]) + dot(pick, bl[n]))[0:8] for n in range(16)]

    total = [zero, zero]

    def use_mapped(n):
        m = qg[n].astype(F32)
        total[0] = total[0] + right_block(n) * m
        total[1] = total[1] + m * m

    collect(qg, r_q, use_mapped)
    step = norm / jnp.sum(total[0], axis=1, keepdims=True)

    size = jnp.sum(total[1], axis=1, keepdims=True)
    beta = jnp.maximum(step * step * size / norm - 1.0, 0.0)

    image = zero
    for n in range(16):
        b = right_block(n)
        close = (b - step * qg[n].astype(F32) + beta * b).astype(BF16)
        at = canon(n // 4, n % 4)
        image = image + dot(close, a_op[at, 0], NT) + dot(close, a_op[at, 1], NT)
        if n == 0:
            mine = close.astype(F32)
    products = [right_block(0) * image, mapped * image, mine * image, jnp.zeros((16, 256), F32)]
    tiny[0] = dot(jnp.ones((8, 256), F32), jnp.concatenate(products, axis=0), NT, lax.Precision.HIGHEST)
    for i, j in others:
        at = (4 - i) % 4 * 4 + (4 - j) % 4
        send(tiny.at[0], tiny.at[at], s_t.at[at], r_t.at[at], plane_peer(i, j))

    for i, j in reversed(others):
        at = 4 * i + j
        arrived(five_in.at[at], r_f.at[at])
    ms = [five_out[0]] + [five_in[n] for n in range(1, 16)]

    def row_sum(parts):
        total = parts[0]
        for part in parts[1:]:
            total = total + part
        return jnp.sum(total, axis=1, keepdims=True)

    norm5 = row_sum([b * b for b in bs])
    step5 = norm5 / row_sum([b * m for b, m in zip(bs, ms)])
    rs = [b - step5 * m for b, m in zip(bs, ms)]
    next5 = row_sum([v * v for v in rs])
    beta5 = next5 / norm5
    ps = [v + beta5 * b for v, b in zip(rs, bs)]

    for i, j in reversed(others):
        at = 4 * i + j
        arrived(tiny.at[at], r_t.at[at])
    sums = tiny[0]
    for n in range(1, 16):
        sums = sums + tiny[n]
    line = lax.broadcasted_iota(jnp.int32, (8, 256), 0)
    column = lax.broadcasted_iota(jnp.int32, (8, 256), 1)

    def five(start):
        return jnp.sum(jnp.where(column == line + (first + start), sums, 0.0), axis=1, keepdims=True)

    curv = 2.0 * ((1.0 + beta5) * five(0) - step5 * five(80)) - five(160)
    step2 = next5 / curv
    for i in range(4):
        for j in range(4):
            n = 4 * i + j
            value = step5 * bs[n] + step2 * ps[n]
            col = pl.multiple_of(block_row(i, j) * 256, 256)
            out_ref[:, pl.ds(col, 256)] = value[0:5]
    for copy in sent:
        copy.wait_send()


def local(silo_grams, silo_weights):
    dma = pltpu.SemaphoreType.DMA
    scratch = [
        pltpu.VMEM((2, 256, 640), BF16),
        pltpu.VMEM((16, 2, 256, 256), F32),
        pltpu.VMEM((2, 4, 80, 512), BF16),
        pltpu.VMEM((16, 4, 80, 256), F32),
        pltpu.VMEM((16, 4, 80, 256), F32),
        pltpu.VMEM((16, 4, 80, 256), F32),
        pltpu.VMEM((2, 2, 4, 80, 256), F32),
        pltpu.VMEM((2, 4, 4, 80, 256), F32),
        pltpu.VMEM((3, 4, 80, 256), F32),
        pltpu.VMEM((3, 80, 256), F32),
        pltpu.VMEM((16, 256, 256), F32),
        pltpu.VMEM((8, 256, 256), F32),
        pltpu.VMEM((2, 256, 256), F32),
        pltpu.VMEM((2, 2, 256, 256), F32),
        pltpu.VMEM((16, 2, 256, 256), BF16),
        pltpu.VMEM((16, 80, 256), BF16),
        pltpu.VMEM((16, 80, 256), BF16),
        pltpu.VMEM((16, 80, 256), BF16),
        pltpu.VMEM((80, 256), F32),
        pltpu.VMEM((16, 8, 256), F32),
        pltpu.VMEM((16, 8, 256), F32),
        pltpu.VMEM((16, 8, 256), F32),
    ]
    counts = [1, 16, 8, 8, 10, 10, 6, 6, 3, 3, 4, 4, 6, 6, 6, 6, 8, 8, 16, 16, 16, 16, 16, 16, 16, 16, 16, 16]
    scratch += [dma((n,)) for n in counts]
    return pl.pallas_call(
        kernel,
        out_shape=jax.ShapeDtypeStruct((5, 4096), F32),
        in_specs=[pl.BlockSpec(memory_space=pl.ANY)] * 2,
        out_specs=pl.BlockSpec(memory_space=pltpu.VMEM),
        scratch_shapes=scratch,
        compiler_params=pltpu.CompilerParams(collective_id=0, has_side_effects=True, vmem_limit_bytes=62 << 20),
        cost_estimate=pl.CostEstimate(flops=6_500_000_000, bytes_accessed=9_200_000, transcendentals=0),
    )(silo_grams, silo_weights)


def solution(mesh):
    torus = Mesh(mesh.devices.reshape(4, 2, 4, 4), AXES)
    silo, row = ("z", "core"), ("y", "x")
    in_specs = (P(silo, row, None), P(silo, row, None))
    out_specs = P(silo + row, None)
    return jax.shard_map(local, mesh=torus, in_specs=in_specs, out_specs=out_specs, check_vma=False)
```

```python
import jax
import jax.numpy as jnp
from jax import lax
from jax.experimental import pallas as pl
from jax.experimental.pallas import tpu as pltpu
from jax.sharding import Mesh
from jax.sharding import PartitionSpec as P

F32, BF16 = jnp.float32, jnp.bfloat16
MESH = pl.DeviceIdType.MESH
AXES = ("z", "core", "y", "x")
NT = (((1,), (1,)), ((), ()))
NN = (((1,), (0,)), ((), ()))
NEAR = (1, 3, 2)
FAR = (2, 1, 3, 0)


def dot(a, b, dims=NN, precision=None):
    return lax.dot_general(a, b, dims, precision=precision, preferred_element_type=F32)


def halves(value):
    high = value.astype(BF16)
    return high, (value - high.astype(F32)).astype(BF16)


def kernel(
    g_hbm, w_hbm, out_ref,
    w_raw, g, wt, p, q, r, far, near, second, third,
    ap, a_sib, a_far, a_near, a_op, bg, bl, qg, acc, five_out, five_in, tiny,
    w_sem, load_sem, s_sib, r_sib, s_one, r_one, s_two, r_two, s_z, r_z,
    s_asib, r_asib, s_ars, r_ars, s_aag, r_aag, s_afw, r_afw,
    s_b, r_b, s_l, r_l, s_q, r_q, s_f, r_f, s_t, r_t,
):
    z, k, y, x = (lax.axis_index(a) for a in AXES)

    def dxy(i, j):
        return (1 - k) * i + k * j, (1 - k) * j + k * i

    def block_row(i, j):
        dx, dy = dxy(i, j)
        return lax.rem(y + dy, 4) * 4 + lax.rem(x + dx, 4)

    def canon(i, j):
        dx, dy = dxy(i, j)
        return dx * 4 + dy

    def plane_peer(i, j):
        dx, dy = dxy(i, j)
        return (z, k, lax.rem(y + dy, 4), lax.rem(x + dx, 4))

    def z_peer(d):
        return (lax.rem(z + d, 4), k, y, x)

    sibling = (z, 1 - k, y, x)

    def remote(src, dst, ssem, rsem, device):
        return pltpu.make_async_remote_copy(src, dst, ssem, rsem, device_id=device, device_id_type=MESH)

    sent = []

    def send(*args):
        copy = remote(*args)
        copy.start()
        sent.append(copy)

    def arrived(dst, rsem):
        remote(dst, dst, s_sib.at[0], rsem, sibling).wait_recv()

    weights = pltpu.make_async_copy(w_hbm, w_raw, w_sem.at[0])
    weights.start()

    def load(i, j):
        col = pl.multiple_of(block_row(i, j) * 256, 256)
        return pltpu.make_async_copy(g_hbm.at[:, :, pl.ds(col, 256)], g.at[4 * i + j], load_sem.at[4 * i + j])

    blocks = [(2, 2), (1, 2), (2, 1), (2, 0), (0, 2), (2, 3), (3, 2), (1, 3), (3, 1), (3, 0), (0, 3)]
    blocks += [(1, 1), (1, 0), (0, 1), (3, 3), (0, 0)]
    for i, j in blocks[:5]:
        load(i, j).start()

    barrier = pltpu.get_barrier_semaphore()
    others = [(i, j) for i in FAR for j in FAR if i or j]
    for i, j in others:
        pl.semaphore_signal(barrier, 1, device_id=plane_peer(i, j), device_id_type=MESH)
    for d in NEAR:
        pl.semaphore_signal(barrier, 1, device_id=z_peer(d), device_id_type=MESH)
    pl.semaphore_signal(barrier, 1, device_id=sibling, device_id_type=MESH)

    weights.wait()
    flipped = w_raw[...].reshape(512, 640).astype(F32).T.astype(BF16)
    for s in range(8):
        wt[lax.rem(s + k, 2), lax.rem(s // 2 + 4 - z, 4)] = flipped[s * 80 : (s + 1) * 80]

    summed = []

    def add_silos(count):
        for i, j in blocks[len(summed) : count]:
            load(i, j).wait()
            ap[canon(i, j)] = g[4 * i + j, 0] + g[4 * i + j, 1]
            summed.append((i, j))

    def tiles(lo, hi):
        add_silos(hi)
        for i, j in blocks[lo:hi]:
            high, low = halves(g[4 * i + j])
            w = wt[...].reshape(640, 512)
            both = dot(w, high.reshape(512, 256)) + dot(w, low.reshape(512, 256))
            p[4 * i + j] = both[:320].reshape(4, 80, 256)
            q[4 * j + i] = both[320:].reshape(4, 80, 256)

    def to_sibling(lo, count, sem):
        rows = pl.ds(lo, count)
        send(q.at[rows], r.at[rows], s_sib.at[sem], r_sib.at[sem], sibling)

    def add_sibling(lo, count, sem):
        rows = pl.ds(lo, count)
        arrived(r.at[rows], r_sib.at[sem])
        for n in range(lo, lo + count):
            p[n] += r[n]

    def quarter(d, n):
        return 2 * lax.rem(z + d, 4) + n

    up, down = plane_peer(1, 0), plane_peer(3, 0)
    z_up, z_down = z_peer(1), z_peer(3)

    for i, j in blocks[5:]:
        load(i, j).start()
    tiles(0, 3)
    pl.semaphore_wait(barrier, 19)
    to_sibling(9, 2, 0)
    tiles(3, 5)
    to_sibling(8, 1, 1)
    add_sibling(9, 2, 0)
    send(p.at[9], far.at[0, 1], s_one.at[0], r_one.at[0], up)
    send(p.at[10], far.at[1, 0], s_one.at[1], r_one.at[1], down)

    def op_to_sibling(d):
        rows = pl.ds(quarter(d, 0), 2)
        send(ap.at[pl.ds(8 * (1 - k) + quarter(d, 0), 2)], a_sib.at[rows], s_asib.at[d], r_asib.at[d], sibling)

    def op_from_sibling(d):
        arrived(a_sib.at[pl.ds(quarter(d, 0), 2)], r_asib.at[d])
        for n in range(2):
            a_sib[quarter(d, n)] += ap[8 * k + quarter(d, n)]

    add_silos(16)
    op_to_sibling(2)
    tiles(5, 7)
    to_sibling(11, 1, 2)
    add_sibling(8, 1, 1)
    send(p.at[8], far.at[0, 0], s_one.at[8], r_one.at[8], up)
    op_from_sibling(2)
    send(a_sib.at[quarter(2, 0)], a_far.at[0], s_ars.at[0], r_ars.at[0], z_up)
    send(a_sib.at[quarter(2, 1)], a_far.at[1], s_ars.at[1], r_ars.at[1], z_down)
    tiles(7, 9)
    add_sibling(11, 1, 2)
    send(p.at[11], far.at[1, 1], s_one.at[9], r_one.at[9], down)
    tiles(9, 11)
    to_sibling(6, 2, 3)
    to_sibling(12, 2, 4)
    op_to_sibling(1)
    op_to_sibling(3)
    tiles(11, 13)
    add_sibling(6, 2, 3)
    send(p.at[pl.ds(6, 2)], near.at[0, pl.ds(2, 2)], s_one.at[2], r_one.at[2], up)
    add_sibling(12, 2, 4)
    send(p.at[pl.ds(12, 2)], near.at[1, pl.ds(0, 2)], s_one.at[3], r_one.at[3], down)
    tiles(13, 15)
    to_sibling(4, 2, 5)
    to_sibling(14, 2, 6)
    op_from_sibling(1)
    send(a_sib.at[quarter(1, 1)], a_near.at[0, 1], s_ars.at[2], r_ars.at[2], z_up)
    op_from_sibling(3)
    send(a_sib.at[quarter(3, 0)], a_near.at[1, 0], s_ars.at[3], r_ars.at[3], z_down)
    tiles(15, 16)
    to_sibling(0, 4, 7)
    op_to_sibling(0)
    add_sibling(4, 2, 5)
    add_sibling(14, 2, 6)

    def relay_up(n, sem):
        arrived(far.at[0, n], r_one.at[sem])
        p[4 + n] += far[0, n]
        send(p.at[4 + n], near.at[0, n], s_one.at[4 + n], r_one.at[4 + n], up)

    def relay_down(n, sem):
        arrived(far.at[1, n], r_one.at[sem])
        p[14 + n] += far[1, n]
        send(p.at[14 + n], near.at[1, 2 + n], s_one.at[6 + n], r_one.at[6 + n], down)

    relay_up(1, 0)
    relay_down(0, 1)
    add_sibling(0, 4, 7)
    relay_up(0, 8)
    relay_down(1, 9)
    arrived(a_far.at[0], r_ars.at[0])
    a_sib[quarter(1, 0)] += a_far[0]
    send(a_sib.at[quarter(1, 0)], a_near.at[0, 0], s_ars.at[4], r_ars.at[4], z_up)
    arrived(a_far.at[1], r_ars.at[1])
    a_sib[quarter(3, 1)] += a_far[1]
    send(a_sib.at[quarter(3, 1)], a_near.at[1, 1], s_ars.at[5], r_ars.at[5], z_down)

    def second_axis(d):
        send(p.at[d, pl.ds(1, 3)], second.at[3 - d, pl.ds(1, 3)], s_two.at[3 - d], r_two.at[3 - d], plane_peer(0, d))
        send(p.at[d, 0], second.at[3 - d, 0], s_two.at[6 - d], r_two.at[6 - d], plane_peer(0, d))

    def whole_sum(n):
        p[n] += near[0, n] + near[1, n]

    arrived(near.at[0, pl.ds(2, 2)], r_one.at[2])
    arrived(near.at[1, pl.ds(0, 2)], r_one.at[3])
    arrived(near.at[0, 1], r_one.at[5])
    whole_sum(1)
    second_axis(1)
    arrived(near.at[1, 2], r_one.at[6])
    whole_sum(2)
    second_axis(2)

    arrived(a_near.at[0, 1], r_ars.at[2])
    arrived(a_near.at[1, 0], r_ars.at[3])
    arrived(a_near.at[0, 0], r_ars.at[4])
    arrived(a_near.at[1, 1], r_ars.at[5])

    def pass_op(at, ssem, rsem, device):
        send(a_op.at[at], a_op.at[at], ssem, rsem, device)

    op_from_sibling(0)
    own = 8 * k + quarter(0, 0)
    for n in range(2):
        high, low = halves(a_sib[quarter(0, n)] + a_near[0, n] + a_near[1, n])
        a_op[own + n, 0] = high
        a_op[own + n, 1] = low
    pass_op(own, s_aag.at[0], r_aag.at[0], z_up)
    pass_op(own + 1, s_aag.at[1], r_aag.at[1], z_down)
    pass_op(own + 1, s_aag.at[2], r_aag.at[2], z_up)
    pass_op(own, s_aag.at[3], r_aag.at[3], z_down)
    arrived(near.at[1, 3], r_one.at[7])
    whole_sum(3)
    second_axis(3)
    arrived(near.at[0, 0], r_one.at[4])
    whole_sum(0)

    for d in NEAR:
        arrived(second.at[3 - d, pl.ds(1, 3)], r_two.at[3 - d])
    for d in NEAR:
        p[0, d] += second[0, d] + second[1, d] + second[2, d]
        send(p.at[0, d], third.at[3 - d], s_z.at[3 - d], r_z.at[3 - d], z_peer(d))
    for d in NEAR:
        arrived(second.at[3 - d, 0], r_two.at[6 - d])
    right = p[0, 0] + second[0, 0] + second[1, 0] + second[2, 0]

    for d in NEAR:
        arrived(third.at[3 - d], r_z.at[3 - d])
    right = right + third[0] + third[1] + third[2]

    def spread(buf, ss, rs):
        for d in NEAR:
            send(buf.at[0], buf.at[16 - 4 * d], ss.at[16 - 4 * d], rs.at[16 - 4 * d], plane_peer(d, 0))
        for d in NEAR:
            send(buf.at[0], buf.at[4 - d], ss.at[4 - d], rs.at[4 - d], plane_peer(0, d))

    def pass_on(buf, ss, rs):
        for i in NEAR:
            arrived(buf.at[4 * i], rs.at[4 * i])
            for d in NEAR:
                at = 4 * i + 4 - d
                send(buf.at[4 * i], buf.at[at], ss.at[at], rs.at[at], plane_peer(0, d))

    def collect(buf, rs, use):
        for i in range(4):
            use(4 * i)
        for i in (0, 1, 3, 2):
            for j in NEAR:
                at = 4 * i + j
                arrived(buf.at[at], rs.at[at])
                use(at)

    def right_block(n):
        return bg[n].astype(F32) + bl[n].astype(F32)

    high, low = halves(right)
    bg[0] = high
    bl[0] = low
    spread(bg, s_b, r_b)

    below, above, across = (8 * k + quarter(d, 0) for d in (3, 1, 2))
    arrived(a_op.at[below], r_aag.at[0])
    pass_op(below, s_aag.at[4], r_aag.at[4], z_up)
    arrived(a_op.at[above + 1], r_aag.at[1])
    pass_op(above + 1, s_aag.at[5], r_aag.at[5], z_down)
    for n in range(2):
        pass_op(own + n, s_afw.at[n], r_afw.at[n], sibling)

    pass_on(bg, s_b, r_b)
    spread(bl, s_l, r_l)

    for at, n in ((below, 0), (above + 1, 1), (below + 1, 2), (above, 3), (across, 4), (across + 1, 5)):
        if n > 1:
            arrived(a_op.at[at], r_aag.at[n])
        pass_op(at, s_afw.at[2 + n], r_afw.at[2 + n], sibling)
    other = 8 * (1 - 2 * k)
    for n, at in enumerate((own, own + 1, below, above + 1, below + 1, above, across, across + 1)):
        arrived(a_op.at[at + other], r_afw.at[n])

    zero = jnp.zeros((80, 256), F32)
    total = [zero]

    def use_high(n):
        at = canon(n // 4, n % 4)
        total[0] = total[0] + dot(bg[n], a_op[at, 0], NT) + dot(bg[n], a_op[at, 1], NT)

    collect(bg, r_b, use_high)
    acc[...] = total[0]
    qg[0] = total[0].astype(BF16)
    spread(qg, s_q, r_q)
    pass_on(bl, s_l, r_l)
    pass_on(qg, s_q, r_q)

    total = [zero]

    def use_low(n):
        total[0] = total[0] + dot(bl[n], a_op[canon(n // 4, n % 4), 0], NT)

    collect(bl, r_l, use_low)
    mapped = acc[...] + total[0]
    norm = zero
    for n in range(16):
        b = right_block(n)
        norm = norm + b * b
    norm = jnp.sum(norm, axis=1, keepdims=True)

    line = lax.broadcasted_iota(jnp.int32, (128, 80), 0)
    column = lax.broadcasted_iota(jnp.int32, (128, 80), 1)
    slot, line = lax.shift_right_logical(line, 3), line & 7
    dx, dy = dxy(lax.shift_right_logical(slot, 2), slot & 3)
    row = ((y + dy) & 3) * 4 + ((x + dx) & 3)
    pick = jnp.where((line < 5) & (column == line + 5 * row), 1.0, 0.0).astype(BF16)
    high, low = halves(mapped)
    five_out[...] = (dot(pick, high) + dot(pick, low)).reshape(16, 8, 256)
    for i, j in others:
        at = (4 - i) % 4 * 4 + (4 - j) % 4
        send(five_out.at[4 * i + j], five_in.at[at], s_f.at[at], r_f.at[at], plane_peer(i, j))

    first = 5 * (4 * y + x)
    line = lax.broadcasted_iota(jnp.int32, (16, 80), 0)
    column = lax.broadcasted_iota(jnp.int32, (16, 80), 1)
    pick = jnp.where((line < 5) & (column == line + first), 1.0, 0.0).astype(BF16)
    bs = [(dot(pick, bg[n]) + dot(pick, bl[n]))[0:8] for n in range(16)]

    total = [zero, zero]

    def use_mapped(n):
        m = qg[n].astype(F32)
        total[0] = total[0] + right_block(n) * m
        total[1] = total[1] + m * m

    collect(qg, r_q, use_mapped)
    step = norm / jnp.sum(total[0], axis=1, keepdims=True)

    size = jnp.sum(total[1], axis=1, keepdims=True)
    beta = jnp.maximum(step * step * size / norm - 1.0, 0.0)

    image = zero
    for n in range(16):
        b = right_block(n)
        close = (b - step * qg[n].astype(F32) + beta * b).astype(BF16)
        at = canon(n // 4, n % 4)
        image = image + dot(close, a_op[at, 0], NT) + dot(close, a_op[at, 1], NT)
        if n == 0:
            mine = close.astype(F32)
    products = [right_block(0) * image, mapped * image, mine * image, jnp.zeros((16, 256), F32)]
    tiny[0] = dot(jnp.ones((8, 256), F32), jnp.concatenate(products, axis=0), NT, lax.Precision.HIGHEST)
    for i, j in others:
        at = (4 - i) % 4 * 4 + (4 - j) % 4
        send(tiny.at[0], tiny.at[at], s_t.at[at], r_t.at[at], plane_peer(i, j))

    for i, j in reversed(others):
        at = 4 * i + j
        arrived(five_in.at[at], r_f.at[at])
    ms = [five_out[0]] + [five_in[n] for n in range(1, 16)]

    def row_sum(parts):
        total = parts[0]
        for part in parts[1:]:
            total = total + part
        return jnp.sum(total, axis=1, keepdims=True)

    norm5 = row_sum([b * b for b in bs])
    step5 = norm5 / row_sum([b * m for b, m in zip(bs, ms)])
    rs = [b - step5 * m for b, m in zip(bs, ms)]
    next5 = row_sum([v * v for v in rs])
    beta5 = next5 / norm5
    ps = [v + beta5 * b for v, b in zip(rs, bs)]

    for i, j in reversed(others):
        at = 4 * i + j
        arrived(tiny.at[at], r_t.at[at])
    sums = tiny[0]
    for n in range(1, 16):
        sums = sums + tiny[n]
    line = lax.broadcasted_iota(jnp.int32, (8, 256), 0)
    column = lax.broadcasted_iota(jnp.int32, (8, 256), 1)

    def five(start):
        return jnp.sum(jnp.where(column == line + (first + start), sums, 0.0), axis=1, keepdims=True)

    curv = 2.0 * ((1.0 + beta5) * five(0) - step5 * five(80)) - five(160)
    step2 = next5 / curv
    for i in range(4):
        for j in range(4):
            n = 4 * i + j
            value = step5 * bs[n] + step2 * ps[n]
            col = pl.multiple_of(block_row(i, j) * 256, 256)
            out_ref[:, pl.ds(col, 256)] = value[0:5]
    for copy in sent:
        copy.wait_send()


def local(silo_grams, silo_weights):
    dma = pltpu.SemaphoreType.DMA
    scratch = [
        pltpu.VMEM((2, 256, 640), BF16),
        pltpu.VMEM((16, 2, 256, 256), F32),
        pltpu.VMEM((2, 4, 80, 512), BF16),
        pltpu.VMEM((16, 4, 80, 256), F32),
        pltpu.VMEM((16, 4, 80, 256), F32),
        pltpu.VMEM((16, 4, 80, 256), F32),
        pltpu.VMEM((2, 2, 4, 80, 256), F32),
        pltpu.VMEM((2, 4, 4, 80, 256), F32),
        pltpu.VMEM((3, 4, 80, 256), F32),
        pltpu.VMEM((3, 80, 256), F32),
        pltpu.VMEM((16, 256, 256), F32),
        pltpu.VMEM((8, 256, 256), F32),
        pltpu.VMEM((2, 256, 256), F32),
        pltpu.VMEM((2, 2, 256, 256), F32),
        pltpu.VMEM((16, 2, 256, 256), BF16),
        pltpu.VMEM((16, 80, 256), BF16),
        pltpu.VMEM((16, 80, 256), BF16),
        pltpu.VMEM((16, 80, 256), BF16),
        pltpu.VMEM((80, 256), F32),
        pltpu.VMEM((16, 8, 256), F32),
        pltpu.VMEM((16, 8, 256), F32),
        pltpu.VMEM((16, 8, 256), F32),
    ]
    counts = [1, 16, 8, 8, 10, 10, 6, 6, 3, 3, 4, 4, 6, 6, 6, 6, 8, 8, 16, 16, 16, 16, 16, 16, 16, 16, 16, 16]
    scratch += [dma((n,)) for n in counts]
    return pl.pallas_call(
        kernel,
        out_shape=jax.ShapeDtypeStruct((5, 4096), F32),
        in_specs=[pl.BlockSpec(memory_space=pl.ANY)] * 2,
        out_specs=pl.BlockSpec(memory_space=pltpu.VMEM),
        scratch_shapes=scratch,
        compiler_params=pltpu.CompilerParams(collective_id=0, has_side_effects=True, vmem_limit_bytes=62 << 20),
        cost_estimate=pl.CostEstimate(flops=6_500_000_000, bytes_accessed=9_200_000, transcendentals=0),
    )(silo_grams, silo_weights)


def solution(mesh):
    torus = Mesh(mesh.devices.reshape(4, 2, 4, 4), AXES)
    silo, row = ("z", "core"), ("y", "x")
    in_specs = (P(silo, row, None), P(silo, row, None))
    out_specs = P(silo + row, None)
    return jax.shard_map(local, mesh=torus, in_specs=in_specs, out_specs=out_specs, check_vma=False)
```

```python
import jax
import jax.numpy as jnp
from jax import lax
from jax.experimental import pallas as pl
from jax.experimental.pallas import tpu as pltpu
from jax.sharding import Mesh
from jax.sharding import PartitionSpec as P

F32, BF16 = jnp.float32, jnp.bfloat16
MESH = pl.DeviceIdType.MESH
AXES = ("z", "core", "y", "x")
NT = (((1,), (1,)), ((), ()))
NN = (((1,), (0,)), ((), ()))
NEAR = (1, 3, 2)
FAR = (2, 1, 3, 0)


def dot(a, b, dims=NN, precision=None):
    return lax.dot_general(a, b, dims, precision=precision, preferred_element_type=F32)


def halves(value):
    high = value.astype(BF16)
    return high, (value - high.astype(F32)).astype(BF16)


def kernel(
    g_hbm, w_hbm, out_ref,
    w_raw, g, wt, p, q, r, far, near, second, third,
    ap, a_sib, a_far, a_near, a_op, bg, bl, qg, acc, five_out, five_in, tiny,
    w_sem, load_sem, s_sib, r_sib, s_one, r_one, s_two, r_two, s_z, r_z,
    s_asib, r_asib, s_ars, r_ars, s_aag, r_aag, s_afw, r_afw,
    s_b, r_b, s_l, r_l, s_q, r_q, s_f, r_f, s_t, r_t,
):
    z, k, y, x = (lax.axis_index(a) for a in AXES)

    def dxy(i, j):
        return (1 - k) * i + k * j, (1 - k) * j + k * i

    def block_row(i, j):
        dx, dy = dxy(i, j)
        return lax.rem(y + dy, 4) * 4 + lax.rem(x + dx, 4)

    def canon(i, j):
        dx, dy = dxy(i, j)
        return dx * 4 + dy

    def plane_peer(i, j):
        dx, dy = dxy(i, j)
        return (z, k, lax.rem(y + dy, 4), lax.rem(x + dx, 4))

    def z_peer(d):
        return (lax.rem(z + d, 4), k, y, x)

    sibling = (z, 1 - k, y, x)

    def remote(src, dst, ssem, rsem, device):
        return pltpu.make_async_remote_copy(src, dst, ssem, rsem, device_id=device, device_id_type=MESH)

    sent = []

    def send(*args):
        copy = remote(*args)
        copy.start()
        sent.append(copy)

    def arrived(dst, rsem):
        remote(dst, dst, s_sib.at[0], rsem, sibling).wait_recv()

    weights = pltpu.make_async_copy(w_hbm, w_raw, w_sem.at[0])
    weights.start()

    def load(i, j):
        col = pl.multiple_of(block_row(i, j) * 256, 256)
        return pltpu.make_async_copy(g_hbm.at[:, :, pl.ds(col, 256)], g.at[4 * i + j], load_sem.at[4 * i + j])

    blocks = [(2, 2), (1, 2), (2, 1), (2, 0), (0, 2), (2, 3), (3, 2), (1, 3), (3, 1), (3, 0), (0, 3)]
    blocks += [(1, 1), (1, 0), (0, 1), (3, 3), (0, 0)]
    for i, j in blocks[:5]:
        load(i, j).start()

    barrier = pltpu.get_barrier_semaphore()
    others = [(i, j) for i in FAR for j in FAR if i or j]
    for i, j in others:
        pl.semaphore_signal(barrier, 1, device_id=plane_peer(i, j), device_id_type=MESH)
    for d in NEAR:
        pl.semaphore_signal(barrier, 1, device_id=z_peer(d), device_id_type=MESH)
    pl.semaphore_signal(barrier, 1, device_id=sibling, device_id_type=MESH)

    weights.wait()
    flipped = w_raw[...].reshape(512, 640).astype(F32).T.astype(BF16)
    for s in range(8):
        wt[lax.rem(s + k, 2), lax.rem(s // 2 + 4 - z, 4)] = flipped[s * 80 : (s + 1) * 80]

    summed = []

    def add_silos(count):
        for i, j in blocks[len(summed) : count]:
            load(i, j).wait()
            ap[canon(i, j)] = g[4 * i + j, 0] + g[4 * i + j, 1]
            summed.append((i, j))

    def tiles(lo, hi):
        add_silos(hi)
        for i, j in blocks[lo:hi]:
            high, low = halves(g[4 * i + j])
            w = wt[...].reshape(640, 512)
            both = dot(w, high.reshape(512, 256)) + dot(w, low.reshape(512, 256))
            p[4 * i + j] = both[:320].reshape(4, 80, 256)
            q[4 * j + i] = both[320:].reshape(4, 80, 256)

    def to_sibling(lo, count, sem):
        rows = pl.ds(lo, count)
        send(q.at[rows], r.at[rows], s_sib.at[sem], r_sib.at[sem], sibling)

    def add_sibling(lo, count, sem):
        rows = pl.ds(lo, count)
        arrived(r.at[rows], r_sib.at[sem])
        for n in range(lo, lo + count):
            p[n] += r[n]

    def quarter(d, n):
        return 2 * lax.rem(z + d, 4) + n

    up, down = plane_peer(1, 0), plane_peer(3, 0)
    z_up, z_down = z_peer(1), z_peer(3)

    for i, j in blocks[5:]:
        load(i, j).start()
    tiles(0, 3)
    pl.semaphore_wait(barrier, 19)
    to_sibling(9, 2, 0)
    tiles(3, 5)
    to_sibling(8, 1, 1)
    add_sibling(9, 2, 0)
    send(p.at[9], far.at[0, 1], s_one.at[0], r_one.at[0], up)
    send(p.at[10], far.at[1, 0], s_one.at[1], r_one.at[1], down)

    def op_to_sibling(d):
        rows = pl.ds(quarter(d, 0), 2)
        send(ap.at[pl.ds(8 * (1 - k) + quarter(d, 0), 2)], a_sib.at[rows], s_asib.at[d], r_asib.at[d], sibling)

    def op_from_sibling(d):
        arrived(a_sib.at[pl.ds(quarter(d, 0), 2)], r_asib.at[d])
        for n in range(2):
            a_sib[quarter(d, n)] += ap[8 * k + quarter(d, n)]

    add_silos(16)
    op_to_sibling(2)
    tiles(5, 7)
    to_sibling(11, 1, 2)
    add_sibling(8, 1, 1)
    send(p.at[8], far.at[0, 0], s_one.at[8], r_one.at[8], up)
    op_from_sibling(2)
    send(a_sib.at[quarter(2, 0)], a_far.at[0], s_ars.at[0], r_ars.at[0], z_up)
    send(a_sib.at[quarter(2, 1)], a_far.at[1], s_ars.at[1], r_ars.at[1], z_down)
    tiles(7, 9)
    add_sibling(11, 1, 2)
    send(p.at[11], far.at[1, 1], s_one.at[9], r_one.at[9], down)
    tiles(9, 11)
    to_sibling(6, 2, 3)
    to_sibling(12, 2, 4)
    op_to_sibling(1)
    op_to_sibling(3)
    tiles(11, 13)
    add_sibling(6, 2, 3)
    send(p.at[pl.ds(6, 2)], near.at[0, pl.ds(2, 2)], s_one.at[2], r_one.at[2], up)
    add_sibling(12, 2, 4)
    send(p.at[pl.ds(12, 2)], near.at[1, pl.ds(0, 2)], s_one.at[3], r_one.at[3], down)
    tiles(13, 15)
    to_sibling(4, 2, 5)
    to_sibling(14, 2, 6)
    op_from_sibling(1)
    send(a_sib.at[quarter(1, 1)], a_near.at[0, 1], s_ars.at[2], r_ars.at[2], z_up)
    op_from_sibling(3)
    send(a_sib.at[quarter(3, 0)], a_near.at[1, 0], s_ars.at[3], r_ars.at[3], z_down)
    tiles(15, 16)
    to_sibling(0, 4, 7)
    op_to_sibling(0)
    add_sibling(4, 2, 5)
    add_sibling(14, 2, 6)

    def relay_up(n, sem):
        arrived(far.at[0, n], r_one.at[sem])
        p[4 + n] += far[0, n]
        send(p.at[4 + n], near.at[0, n], s_one.at[4 + n], r_one.at[4 + n], up)

    def relay_down(n, sem):
        arrived(far.at[1, n], r_one.at[sem])
        p[14 + n] += far[1, n]
        send(p.at[14 + n], near.at[1, 2 + n], s_one.at[6 + n], r_one.at[6 + n], down)

    relay_up(1, 0)
    relay_down(0, 1)
    add_sibling(0, 4, 7)
    relay_up(0, 8)
    relay_down(1, 9)
    arrived(a_far.at[0], r_ars.at[0])
    a_sib[quarter(1, 0)] += a_far[0]
    send(a_sib.at[quarter(1, 0)], a_near.at[0, 0], s_ars.at[4], r_ars.at[4], z_up)
    arrived(a_far.at[1], r_ars.at[1])
    a_sib[quarter(3, 1)] += a_far[1]
    send(a_sib.at[quarter(3, 1)], a_near.at[1, 1], s_ars.at[5], r_ars.at[5], z_down)

    def second_axis(d):
        send(p.at[d, pl.ds(1, 3)], second.at[3 - d, pl.ds(1, 3)], s_two.at[3 - d], r_two.at[3 - d], plane_peer(0, d))
        send(p.at[d, 0], second.at[3 - d, 0], s_two.at[6 - d], r_two.at[6 - d], plane_peer(0, d))

    def whole_sum(n):
        p[n] += near[0, n] + near[1, n]

    arrived(near.at[0, pl.ds(2, 2)], r_one.at[2])
    arrived(near.at[1, pl.ds(0, 2)], r_one.at[3])
    arrived(near.at[0, 1], r_one.at[5])
    whole_sum(1)
    second_axis(1)
    arrived(near.at[1, 2], r_one.at[6])
    whole_sum(2)
    second_axis(2)

    arrived(a_near.at[0, 1], r_ars.at[2])
    arrived(a_near.at[1, 0], r_ars.at[3])
    arrived(a_near.at[0, 0], r_ars.at[4])
    arrived(a_near.at[1, 1], r_ars.at[5])

    def pass_op(at, ssem, rsem, device):
        send(a_op.at[at], a_op.at[at], ssem, rsem, device)

    op_from_sibling(0)
    own = 8 * k + quarter(0, 0)
    for n in range(2):
        high, low = halves(a_sib[quarter(0, n)] + a_near[0, n] + a_near[1, n])
        a_op[own + n, 0] = high
        a_op[own + n, 1] = low
    pass_op(own, s_aag.at[0], r_aag.at[0], z_up)
    pass_op(own + 1, s_aag.at[1], r_aag.at[1], z_down)
    pass_op(own + 1, s_aag.at[2], r_aag.at[2], z_up)
    pass_op(own, s_aag.at[3], r_aag.at[3], z_down)
    for n in range(2):
        pass_op(own + n, s_afw.at[n], r_afw.at[n], sibling)
    arrived(near.at[1, 3], r_one.at[7])
    whole_sum(3)
    second_axis(3)
    arrived(near.at[0, 0], r_one.at[4])
    whole_sum(0)

    for d in NEAR:
        arrived(second.at[3 - d, pl.ds(1, 3)], r_two.at[3 - d])
    for d in NEAR:
        p[0, d] += second[0, d] + second[1, d] + second[2, d]
        send(p.at[0, d], third.at[3 - d], s_z.at[3 - d], r_z.at[3 - d], z_peer(d))
    for d in NEAR:
        arrived(second.at[3 - d, 0], r_two.at[6 - d])
    right = p[0, 0] + second[0, 0] + second[1, 0] + second[2, 0]

    for d in NEAR:
        arrived(third.at[3 - d], r_z.at[3 - d])
    right = right + third[0] + third[1] + third[2]

    def spread(buf, ss, rs):
        for d in NEAR:
            send(buf.at[0], buf.at[16 - 4 * d], ss.at[16 - 4 * d], rs.at[16 - 4 * d], plane_peer(d, 0))
        for d in NEAR:
            send(buf.at[0], buf.at[4 - d], ss.at[4 - d], rs.at[4 - d], plane_peer(0, d))

    def pass_on(buf, ss, rs):
        for i in NEAR:
            arrived(buf.at[4 * i], rs.at[4 * i])
            for d in NEAR:
                at = 4 * i + 4 - d
                send(buf.at[4 * i], buf.at[at], ss.at[at], rs.at[at], plane_peer(0, d))

    def collect(buf, rs, use):
        for i in range(4):
            use(4 * i)
        for i in (0, 1, 3, 2):
            for j in NEAR:
                at = 4 * i + j
                arrived(buf.at[at], rs.at[at])
                use(at)

    def right_block(n):
        return bg[n].astype(F32) + bl[n].astype(F32)

    high, low = halves(right)
    bg[0] = high
    bl[0] = low
    spread(bg, s_b, r_b)

    below, above, across = (8 * k + quarter(d, 0) for d in (3, 1, 2))
    arrived(a_op.at[below], r_aag.at[0])
    pass_op(below, s_aag.at[4], r_aag.at[4], z_up)
    arrived(a_op.at[above + 1], r_aag.at[1])
    pass_op(above + 1, s_aag.at[5], r_aag.at[5], z_down)

    pass_on(bg, s_b, r_b)
    spread(bl, s_l, r_l)

    for at, n in ((below, 0), (above + 1, 1), (below + 1, 2), (above, 3), (across, 4), (across + 1, 5)):
        if n > 1:
            arrived(a_op.at[at], r_aag.at[n])
        pass_op(at, s_afw.at[2 + n], r_afw.at[2 + n], sibling)
    other = 8 * (1 - 2 * k)
    for n, at in enumerate((own, own + 1, below, above + 1, below + 1, above, across, across + 1)):
        arrived(a_op.at[at + other], r_afw.at[n])

    zero = jnp.zeros((80, 256), F32)
    total = [zero]

    def use_high(n):
        at = canon(n // 4, n % 4)
        total[0] = total[0] + dot(bg[n], a_op[at, 0], NT) + dot(bg[n], a_op[at, 1], NT)

    collect(bg, r_b, use_high)
    acc[...] = total[0]
    qg[0] = total[0].astype(BF16)
    spread(qg, s_q, r_q)
    pass_on(bl, s_l, r_l)
    pass_on(qg, s_q, r_q)

    total = [zero]

    def use_low(n):
        total[0] = total[0] + dot(bl[n], a_op[canon(n // 4, n % 4), 0], NT)

    collect(bl, r_l, use_low)
    mapped = acc[...] + total[0]
    norm = zero
    for n in range(16):
        b = right_block(n)
        norm = norm + b * b
    norm = jnp.sum(norm, axis=1, keepdims=True)

    line = lax.broadcasted_iota(jnp.int32, (128, 80), 0)
    column = lax.broadcasted_iota(jnp.int32, (128, 80), 1)
    slot, line = lax.shift_right_logical(line, 3), line & 7
    dx, dy = dxy(lax.shift_right_logical(slot, 2), slot & 3)
    row = ((y + dy) & 3) * 4 + ((x + dx) & 3)
    pick = jnp.where((line < 5) & (column == line + 5 * row), 1.0, 0.0).astype(BF16)
    high, low = halves(mapped)
    five_out[...] = (dot(pick, high) + dot(pick, low)).reshape(16, 8, 256)
    for i, j in others:
        at = (4 - i) % 4 * 4 + (4 - j) % 4
        send(five_out.at[4 * i + j], five_in.at[at], s_f.at[at], r_f.at[at], plane_peer(i, j))

    first = 5 * (4 * y + x)
    line = lax.broadcasted_iota(jnp.int32, (16, 80), 0)
    column = lax.broadcasted_iota(jnp.int32, (16, 80), 1)
    pick = jnp.where((line < 5) & (column == line + first), 1.0, 0.0).astype(BF16)
    bs = [(dot(pick, bg[n]) + dot(pick, bl[n]))[0:8] for n in range(16)]

    total = [zero, zero]

    def use_mapped(n):
        m = qg[n].astype(F32)
        total[0] = total[0] + right_block(n) * m
        total[1] = total[1] + m * m

    collect(qg, r_q, use_mapped)
    step = norm / jnp.sum(total[0], axis=1, keepdims=True)

    size = jnp.sum(total[1], axis=1, keepdims=True)
    beta = jnp.maximum(step * step * size / norm - 1.0, 0.0)

    image = zero
    for n in range(16):
        b = right_block(n)
        close = (b - step * qg[n].astype(F32) + beta * b).astype(BF16)
        at = canon(n // 4, n % 4)
        image = image + dot(close, a_op[at, 0], NT) + dot(close, a_op[at, 1], NT)
        if n == 0:
            mine = close.astype(F32)
    products = [right_block(0) * image, mapped * image, mine * image, jnp.zeros((16, 256), F32)]
    tiny[0] = dot(jnp.ones((8, 256), F32), jnp.concatenate(products, axis=0), NT, lax.Precision.HIGHEST)
    for i, j in others:
        at = (4 - i) % 4 * 4 + (4 - j) % 4
        send(tiny.at[0], tiny.at[at], s_t.at[at], r_t.at[at], plane_peer(i, j))

    for i, j in reversed(others):
        at = 4 * i + j
        arrived(five_in.at[at], r_f.at[at])
    ms = [five_out[0]] + [five_in[n] for n in range(1, 16)]

    def row_sum(parts):
        total = parts[0]
        for part in parts[1:]:
            total = total + part
        return jnp.sum(total, axis=1, keepdims=True)

    norm5 = row_sum([b * b for b in bs])
    step5 = norm5 / row_sum([b * m for b, m in zip(bs, ms)])
    rs = [b - step5 * m for b, m in zip(bs, ms)]
    next5 = row_sum([v * v for v in rs])
    beta5 = next5 / norm5
    ps = [v + beta5 * b for v, b in zip(rs, bs)]

    for i, j in reversed(others):
        at = 4 * i + j
        arrived(tiny.at[at], r_t.at[at])
    sums = tiny[0]
    for n in range(1, 16):
        sums = sums + tiny[n]
    line = lax.broadcasted_iota(jnp.int32, (8, 256), 0)
    column = lax.broadcasted_iota(jnp.int32, (8, 256), 1)

    def five(start):
        return jnp.sum(jnp.where(column == line + (first + start), sums, 0.0), axis=1, keepdims=True)

    curv = 2.0 * ((1.0 + beta5) * five(0) - step5 * five(80)) - five(160)
    step2 = next5 / curv
    for i in range(4):
        for j in range(4):
            n = 4 * i + j
            value = step5 * bs[n] + step2 * ps[n]
            col = pl.multiple_of(block_row(i, j) * 256, 256)
            out_ref[:, pl.ds(col, 256)] = value[0:5]
    for copy in sent:
        copy.wait_send()


def local(silo_grams, silo_weights):
    dma = pltpu.SemaphoreType.DMA
    scratch = [
        pltpu.VMEM((2, 256, 640), BF16),
        pltpu.VMEM((16, 2, 256, 256), F32),
        pltpu.VMEM((2, 4, 80, 512), BF16),
        pltpu.VMEM((16, 4, 80, 256), F32),
        pltpu.VMEM((16, 4, 80, 256), F32),
        pltpu.VMEM((16, 4, 80, 256), F32),
        pltpu.VMEM((2, 2, 4, 80, 256), F32),
        pltpu.VMEM((2, 4, 4, 80, 256), F32),
        pltpu.VMEM((3, 4, 80, 256), F32),
        pltpu.VMEM((3, 80, 256), F32),
        pltpu.VMEM((16, 256, 256), F32),
        pltpu.VMEM((8, 256, 256), F32),
        pltpu.VMEM((2, 256, 256), F32),
        pltpu.VMEM((2, 2, 256, 256), F32),
        pltpu.VMEM((16, 2, 256, 256), BF16),
        pltpu.VMEM((16, 80, 256), BF16),
        pltpu.VMEM((16, 80, 256), BF16),
        pltpu.VMEM((16, 80, 256), BF16),
        pltpu.VMEM((80, 256), F32),
        pltpu.VMEM((16, 8, 256), F32),
        pltpu.VMEM((16, 8, 256), F32),
        pltpu.VMEM((16, 8, 256), F32),
    ]
    counts = [1, 16, 8, 8, 10, 10, 6, 6, 3, 3, 4, 4, 6, 6, 6, 6, 8, 8, 16, 16, 16, 16, 16, 16, 16, 16, 16, 16]
    scratch += [dma((n,)) for n in counts]
    return pl.pallas_call(
        kernel,
        out_shape=jax.ShapeDtypeStruct((5, 4096), F32),
        in_specs=[pl.BlockSpec(memory_space=pl.ANY)] * 2,
        out_specs=pl.BlockSpec(memory_space=pltpu.VMEM),
        scratch_shapes=scratch,
        compiler_params=pltpu.CompilerParams(collective_id=0, has_side_effects=True, vmem_limit_bytes=62 << 20),
        cost_estimate=pl.CostEstimate(flops=6_500_000_000, bytes_accessed=9_200_000, transcendentals=0),
    )(silo_grams, silo_weights)


def solution(mesh):
    torus = Mesh(mesh.devices.reshape(4, 2, 4, 4), AXES)
    silo, row = ("z", "core"), ("y", "x")
    in_specs = (P(silo, row, None), P(silo, row, None))
    out_specs = P(silo + row, None)
    return jax.shard_map(local, mesh=torus, in_specs=in_specs, out_specs=out_specs, check_vma=False)
```
